32 devices in a mesh: gx: 4 (over x, core), gy: 8 (over z, y).
Axes of the slice: x: 2, y: 2, z: 4, core: 2. Of those that a mesh axis runs over, the one named last changes fastest.
Arguments:
- thickness: float32 [8, 512, 1024], P(None, 'gy', 'gx'), may hold values from 1 to 2
- velocity: float32 [2, 8, 512, 1024], P(None, None, 'gy', 'gx'), may hold values from -3 to 3
- bottom: float32 [512, 1024], P('gy', 'gx'), may hold values from -2 to 2
- coriolis: float32 [512, 1024], P('gy', 'gx'), may hold values from -4 to 4
- reduced: float32 [8], replicated, may hold values from 0.2 to 2
Outputs:
- thickness_new: float32 [8, 512, 1024], P(None, 'gy', 'gx')
- velocity_new: float32 [2, 8, 512, 1024], P(None, None, 'gy', 'gx')
The draws below stay inside these ranges and needn't reach their ends.
All inputs are finite; a program needn't handle non-finite values.
Results may differ from the reference program's by a relative error of at most 0.00002.
Values sent between devices are 32-bit elements; how exact they have to be, the bound alone decides.
A program may use at most 128 MiB of HBM per device.

```python
import math
import jax
import jax.numpy as jnp

LEV = 8
NX = 1024
NY = 512


def shard_levels(key, dims, shards, smallest, high):
    level, own = 1.0, jax.random.fold_in(key, 6)
    for dim, parts in shards:
        heights = jnp.exp(jax.random.uniform(jax.random.fold_in(own, dim), (parts,), jnp.float32, smallest / len(shards), high / len(shards)))
        level = level * jnp.repeat(heights, dims[dim] // parts).reshape([-1 if axis == dim else 1 for axis in range(len(dims))])
    return level


def bell_draw(stream_key, shape, spread, limit, pieces=(), held_as=jnp.bfloat16):
    factor_of = shard_levels(stream_key, shape, pieces, -0.22, 0.18) if pieces else 1.0
    values = jax.random.normal(stream_key, shape, jnp.float32) * spread * factor_of
    return jnp.minimum(jnp.maximum(values, -limit), limit).astype(held_as)


def setup_inputs(seed: int = 0) -> dict:
    key_of = jax.random.split(jax.random.key(seed), 6)
    thickness = jnp.clip(1.0 + 1.0 * jax.random.uniform(key_of[0], (LEV, NY, NX), jnp.float32) ** shard_levels(key_of[0], (LEV, NY, NX), ((1, 8), (2, 4)), -0.2, 0.2), 1.0, 2.0)
    velocity = bell_draw(key_of[1], (2, LEV, NY, NX), 0.3, 3.0, ((2, 8), (3, 4)), jnp.float32)
    bottom = jnp.clip(jax.random.uniform(key_of[2], (NY, NX), jnp.float32, -2.0, 2.0) * shard_levels(key_of[2], (NY, NX), ((0, 8), (1, 4)), -0.4, 0.0), -2.0, 2.0)
    coriolis = jnp.clip(jax.random.uniform(key_of[3], (NY, NX), jnp.float32, -4.0, 4.0) * shard_levels(key_of[3], (NY, NX), ((0, 8), (1, 4)), -0.4, 0.0), -4.0, 4.0)
    reduced = jnp.clip(jnp.exp(jax.random.uniform(key_of[4], (LEV,), jnp.float32, math.log(0.2), math.log(2.0))), 0.2, 2.0)
    return {"thickness": thickness, "velocity": velocity, "bottom": bottom, "coriolis": coriolis, "reduced": reduced}


gravity = 0.5
time_step = 0.1
half_step = 0.05


def eastward(values):
    return jnp.roll(values, -1, axis=-1)


def westward(values):
    return jnp.roll(values, 1, axis=-1)


def northward(values):
    return jnp.roll(values, -1, axis=-2)


def southward(values):
    return jnp.roll(values, 1, axis=-2)


def tendency(thick, along_x, along_y, bottom, coriolis, reduced):
    flux_x = 0.5 * (thick + eastward(thick)) * along_x
    flux_y = 0.5 * (thick + northward(thick)) * along_y
    vorticity = (eastward(along_y) - along_y) - (northward(along_x) - along_x)
    thick_vertex = 0.25 * (thick + eastward(thick) + northward(thick) + eastward(northward(thick)))
    potential = (vorticity + coriolis) / thick_vertex
    kinetic = 0.25 * (along_x * along_x + westward(along_x) * westward(along_x) + along_y * along_y + southward(along_y) * southward(along_y))
    pressure = gravity * (bottom + jnp.sum(thick, axis=0)) + reduced[:, None, None] * thick
    bernoulli = kinetic + pressure
    rate_thick = -((flux_x - westward(flux_x)) + (flux_y - southward(flux_y)))
    north_flux = potential * (0.5 * (flux_y + eastward(flux_y)))
    rate_x = 0.5 * (southward(north_flux) + north_flux) - (eastward(bernoulli) - bernoulli)
    east_flux = potential * (0.5 * (flux_x + northward(flux_x)))
    rate_y = -0.5 * (westward(east_flux) + east_flux) - (northward(bernoulli) - bernoulli)
    return rate_thick, rate_x, rate_y


def extend(values):
    wrapped = jnp.concatenate([values[..., -1:, :], values, values[..., :1, :]], axis=-2)
    widths = [(0, 0)] * (values.ndim - 1) + [(1, 1)]
    return jnp.pad(wrapped, widths)


def crop(values):
    return values[..., 1:-1, 1:-1]


def reference(thickness, velocity, bottom, coriolis, reduced):
    position = jnp.arange(NX, dtype=jnp.int32)
    wall_x = (position < NX - 1).astype(jnp.float32)
    thick_start = thickness
    east_start = velocity[0] * wall_x
    north_start = velocity[1]
    bottom_edge = extend(bottom)
    coriolis_edge = extend(coriolis)

    def rates(thick, along_x, along_y):
        result = tendency(extend(thick), extend(along_x), extend(along_y), bottom_edge, coriolis_edge, reduced)
        return [crop(item) for item in result]

    first = rates(thick_start, east_start, north_start)
    thick_mid = thick_start + time_step * first[0]
    east_mid = (east_start + time_step * first[1]) * wall_x
    north_mid = north_start + time_step * first[2]
    second = rates(thick_mid, east_mid, north_mid)
    thick_end = thick_start + half_step * (first[0] + second[0])
    east_end = (east_start + half_step * (first[1] + second[1])) * wall_x
    north_end = north_start + half_step * (first[2] + second[2])
    return thick_end, jnp.stack([east_end, north_end])
```

```python
import jax
import jax.numpy as jnp
from jax import lax
from jax.experimental import pallas as pl
from jax.experimental.pallas import tpu as pltpu
from jax.sharding import PartitionSpec as P

time_step = 0.1
LANES = 128
SUB = 8
GROUP = 16
MESH = pl.DeviceIdType.MESH


def kernel(
    count_x, count_y, rows,
    h_in, vel_in, bottom_in, coriolis_in, reduced_in,
    h_out, vel_out,
    own, mid, result, edge_send, edge_recv, fixed, strip, strip_mid, pack, west_pack, east_pack,
    load_sem, store_sem, send_sem, recv_sem,
):
    levels = SUB
    blocks = rows // SUB
    ext = rows + 2 * SUB
    me_x = lax.axis_index("gx")
    me_y = lax.axis_index("gy")
    west_open = me_x > 0
    east_open = me_x < count_x - 1
    north = lax.rem(me_y + 1, count_y)
    south = lax.rem(me_y + count_y - 1, count_y)

    loads = []
    for half in range(2):
        cols = pl.ds(half * LANES, LANES)
        sources = [h_in.at[:, :, cols], vel_in.at[0, :, :, cols], vel_in.at[1, :, :, cols]]
        for item in range(3):
            loads.append(pltpu.make_async_copy(sources[item], own.at[item, half], load_sem.at[half, item]))
        for item, source in enumerate((bottom_in, coriolis_in)):
            loads.append(
                pltpu.make_async_copy(
                    source.at[:, cols], fixed.at[item, half, pl.ds(SUB, rows)], load_sem.at[half, 3 + item]
                )
            )
    for copy in loads:
        copy.start()

    barrier = pltpu.get_barrier_semaphore()

    def greet(x, y):
        pl.semaphore_signal(barrier, inc=1, device_id={"gx": x, "gy": y}, device_id_type=MESH)

    greet(me_x, north)
    greet(me_x, south)

    @pl.when(west_open)
    def _():
        for y in (north, me_y, south):
            greet(me_x - 1, y)

    @pl.when(east_open)
    def _():
        for y in (north, me_y, south):
            greet(me_x + 1, y)

    @pl.when(jnp.logical_not(west_open))
    def _():
        west_pack[...] = jnp.zeros_like(west_pack)

    @pl.when(jnp.logical_not(east_open))
    def _():
        east_pack[...] = jnp.zeros_like(east_pack)

    lane = lax.broadcasted_iota(jnp.int32, (SUB, LANES), 1)
    sub = lax.broadcasted_iota(jnp.int32, (SUB, LANES), 0)
    level = lane // GROUP
    place = lane - level * GROUP
    reduced_main = jnp.zeros((SUB, LANES), jnp.float32)
    reduced_strip = jnp.zeros((SUB, LANES), jnp.float32)
    for item in range(levels):
        value = 2.0 * reduced_in[item]
        reduced_main = jnp.where(sub == item, value, reduced_main)
        reduced_strip = jnp.where(level == item, value, reduced_strip)

    for copy in loads:
        copy.wait()

    def turn(values, shift):
        return pltpu.roll(values, shift % LANES, 1)

    flat = [[own.at[item, half].reshape(levels * rows, LANES) for half in range(2)] for item in range(3)]

    def own_row(item, half, row):
        return flat[item][half][pl.ds(row, levels, stride=rows), :]

    for item in range(3):
        for half in range(2):
            for row in range(2):
                edge_send[0, item, half, row] = own_row(item, half, rows - 2 + row)
                edge_send[1, item, half, row] = own_row(item, half, row)

    wall_last = jnp.logical_and(place == 13, jnp.logical_not(east_open))

    def spread(gathered):
        left = turn(gathered, -6)
        right = turn(gathered, 6)
        return jnp.where(place < 8, left, right)

    def build(block, _):
        base = pl.multiple_of(block * SUB, SUB)
        after = pl.multiple_of(block * SUB + SUB, SUB)
        made = []
        for item in range(3):
            gathered = jnp.zeros((SUB, LANES), jnp.float32)
            for lev in range(levels):
                low = own[item, 0, lev, pl.ds(base, SUB), :]
                high = own[item, 1, lev, pl.ds(base, SUB), :]
                joined = jnp.where(lane < LANES // 2, low, high)
                gathered = jnp.where(level == lev, turn(joined, GROUP * lev + 8), gathered)
            value = spread(gathered)
            if item == 1:
                value = jnp.where(wall_last, 0.0, value)
            made.append(value)
        for item in range(2):
            low = fixed[item, 0, pl.ds(after, SUB), :]
            high = fixed[item, 1, pl.ds(after, SUB), :]
            joined = turn(jnp.where(lane < LANES // 2, low, high), 8)
            gathered = jnp.where(lane < GROUP, joined, 0.0)
            for shift in (16, 32, 64):
                gathered = gathered + turn(gathered, shift)
            made.append(spread(gathered))
        for item in range(5):
            strip[item, pl.ds(after, SUB), :] = made[item]
        eastbound = turn(made[4], -4)
        westbound = turn(made[4], 4)
        for item in (3, 2, 1, 0):
            eastbound = jnp.where(place < 2 * item + 2, turn(made[item], 2 * item - 12), eastbound)
            westbound = jnp.where(place >= 14 - 2 * item, turn(made[item], 12 - 2 * item), westbound)
        pack[0, pl.ds(base, SUB), :] = eastbound
        pack[1, pl.ds(base, SUB), :] = westbound
        return 0

    lax.fori_loop(0, blocks, build, 0)

    first = pl.ds(0, SUB)
    last = pl.ds(rows - SUB, SUB)
    own_first = pl.ds(SUB, SUB)
    own_last = pl.ds(rows, SUB)
    ext_last = pl.ds(rows + SUB, SUB)
    ext_own = pl.ds(SUB, rows)

    def remote(index, source, target, x, y):
        return pltpu.make_async_remote_copy(
            src_ref=source,
            dst_ref=target,
            send_sem=send_sem.at[index],
            recv_sem=recv_sem.at[index],
            device_id={"gx": x, "gy": y},
            device_id_type=MESH,
        )

    along_y = [
        remote(0, edge_send.at[0], edge_recv.at[0], me_x, north),
        remote(1, edge_send.at[1], edge_recv.at[1], me_x, south),
        remote(2, fixed.at[:, :, own_last], fixed.at[:, :, first], me_x, north),
        remote(3, fixed.at[:, :, own_first], fixed.at[:, :, ext_last], me_x, south),
        remote(4, strip.at[:, own_last], strip.at[:, first], me_x, north),
        remote(5, strip.at[:, own_first], strip.at[:, ext_last], me_x, south),
    ]
    to_east = [
        remote(6, pack.at[0], west_pack.at[ext_own], me_x + 1, me_y),
        remote(7, pack.at[0, last], west_pack.at[first], me_x + 1, north),
        remote(8, pack.at[0, first], west_pack.at[ext_last], me_x + 1, south),
    ]
    to_west = [
        remote(9, pack.at[1], east_pack.at[ext_own], me_x - 1, me_y),
        remote(10, pack.at[1, last], east_pack.at[first], me_x - 1, north),
        remote(11, pack.at[1, first], east_pack.at[ext_last], me_x - 1, south),
    ]

    greeted = 2 + 3 * west_open.astype(jnp.int32) + 3 * east_open.astype(jnp.int32)
    pl.semaphore_wait(barrier, greeted)
    for copy in along_y:
        copy.start()

    @pl.when(east_open)
    def _():
        for copy in to_east:
            copy.start()

    @pl.when(west_open)
    def _():
        for copy in to_west:
            copy.start()

    before_end = lane < LANES - 1
    at_start = lane == 0

    def eastward(pair):
        low, high = turn(pair[0], -1), turn(pair[1], -1)
        return [jnp.where(before_end, low, high), high]

    def westward(pair):
        low, high = turn(pair[0], 1), turn(pair[1], 1)
        return [low, jnp.where(at_start, low, high)]

    def each(function, *pairs):
        return [function(*items) for items in zip(*pairs)]

    def begin(row):
        thick, along_x, along_y = row
        wide = each(lambda a, b: a + b, thick, eastward(thick))
        flux = each(lambda a, b: a * b, wide, along_x)
        zero = [jnp.zeros((SUB, LANES), jnp.float32)] * 2
        return [thick, along_x, along_y, wide, flux, zero, zero, zero]

    def advance(carry, following, bottom_next, coriolis):
        thick, along_x, along_y, wide, flux, bern, flux_y_before, turn_before = carry
        thick_n, along_x_n, along_y_n = following
        wide_n = each(lambda a, b: a + b, thick_n, eastward(thick_n))
        flux_n = each(lambda a, b: a * b, wide_n, along_x_n)
        flux_y = each(lambda a, b, c: (a + b) * c, thick, thick_n, along_y)
        vort = each(
            lambda e, v, un, u, f: (e - v) - (un - u) + f,
            eastward(along_y), along_y, along_x_n, along_x, coriolis,
        )
        spin = each(lambda z, a, b: z / (a + b), vort, wide, wide_n)
        turn_y = each(lambda w, a, b: w * (a + b), spin, flux_y, eastward(flux_y))
        turn_x = each(lambda w, a, b: w * (a + b), spin, flux, flux_n)
        square = each(lambda a: a * a, along_x_n)
        bern_n = each(
            lambda s, w, vn, v, b, h: 0.5 * ((s + w) + (vn * vn + v * v))
            + (b + jnp.sum(h, axis=0, keepdims=True))
            + reduced_main * h,
            square, westward(square), along_y_n, along_y, bottom_next, thick_n,
        )
        rate_h = each(
            lambda f, w, g, p: -((f - w) + (g - p)), flux, westward(flux), flux_y, flux_y_before
        )
        rate_u = each(lambda p, t, e, b: (p + t) - (e - b), turn_before, turn_y, eastward(bern), bern)
        rate_v = each(lambda w, t, n, b: -(w + t) - (n - b), westward(turn_x), turn_x, bern_n, bern)
        carry = [thick_n, along_x_n, along_y_n, wide_n, flux_n, bern_n, flux_y, turn_y]
        return carry, [rate_h, rate_u, rate_v]

    def fixed_row(item, row):
        return [
            jnp.broadcast_to(fixed[item, half, pl.ds(row + SUB, 1), :], (SUB, LANES)) for half in range(2)
        ]

    def start_row(row):
        return [[own_row(item, half, row) for half in range(2)] for item in range(3)]

    def halo_row(side, row):
        return [[edge_recv[side, item, half, row] for half in range(2)] for item in range(3)]

    def mid_row(row):
        return [[mid[item, half, row + 1] for half in range(2)] for item in range(3)]

    def keep_mid(row, carry, rates):
        for item in range(3):
            for half in range(2):
                mid[item, half, row + 1] = carry[item][half] + 0.5 * time_step * rates[item][half]

    def first_step(carry, row, following):
        after, rates = advance(carry, following, fixed_row(0, row + 1), fixed_row(1, row))
        keep_mid(row, carry, rates)
        return after

    carry = begin(start_row(0))
    carry, _ = advance(carry, start_row(1), fixed_row(0, 1), fixed_row(1, 0))
    inner = rows - 2
    unroll = SUB
    whole = inner // unroll

    def first_block(block, carry):
        for step in range(unroll):
            row = block * unroll + step + 1
            carry = first_step(carry, row, start_row(row + 1))
        return carry

    carry = lax.fori_loop(0, whole, first_block, carry)
    for row in range(whole * unroll + 1, inner + 1):
        carry = first_step(carry, row, start_row(row + 1))

    for copy in along_y[:4]:
        copy.wait_recv()
    south_rows = [halo_row(0, 0), halo_row(0, 1), start_row(0), start_row(1)]
    carry = begin(south_rows[0])
    carry, _ = advance(carry, south_rows[1], fixed_row(0, -1), fixed_row(1, -2))
    for row in (-1, 0):
        carry = first_step(carry, row, south_rows[row + 3])
    north_rows = [start_row(rows - 2), start_row(rows - 1), halo_row(1, 0), halo_row(1, 1)]
    carry = begin(north_rows[0])
    carry, _ = advance(carry, north_rows[1], fixed_row(0, rows - 1), fixed_row(1, rows - 2))
    for step in range(2):
        carry = first_step(carry, rows - 1 + step, north_rows[step + 2])

    out_flat = [[result.at[item, half].reshape(levels * rows, LANES) for half in range(2)] for item in range(3)]

    def second_block(block, carry):
        for step in range(unroll):
            row = block * unroll + step
            after, rates = advance(carry, mid_row(row + 1), fixed_row(0, row + 1), fixed_row(1, row))
            start = start_row(row)
            for item in range(3):
                for half in range(2):
                    value = 0.5 * (start[item][half] + carry[item][half]) + 0.25 * time_step * rates[item][half]
                    out_flat[item][half][pl.ds(row, levels, stride=rows), :] = value
            carry = after
        return carry

    carry = begin(mid_row(-1))
    carry, _ = advance(carry, mid_row(0), fixed_row(0, 0), fixed_row(1, -1))
    lax.fori_loop(0, blocks, second_block, carry)

    for copy in along_y[4:]:
        copy.wait_recv()

    @pl.when(west_open)
    def _():
        for copy in to_east:
            copy.wait_recv()

    @pl.when(east_open)
    def _():
        for copy in to_west:
            copy.wait_recv()

    wide_lane = lax.broadcasted_iota(jnp.int32, (ext, LANES), 1)
    wide_place = wide_lane - (wide_lane // GROUP) * GROUP
    from_west = wide_place < 2
    from_east = wide_place >= 14
    outside = jnp.logical_or(
        jnp.logical_and(from_west, jnp.logical_not(west_open)),
        jnp.logical_and(from_east, jnp.logical_not(east_open)),
    )
    closed = jnp.logical_or(outside, jnp.logical_and(wide_place == 13, jnp.logical_not(east_open)))
    received_west = west_pack[...]
    received_east = east_pack[...]
    fields = []
    for item in range(5):
        value = jnp.where(from_west, turn(received_west, -2 * item), strip[item])
        fields.append(jnp.where(from_east, turn(received_east, 2 * item), value))
    weight = jnp.concatenate([reduced_strip] * (ext // SUB), axis=0)

    def strip_rates(thick, along_x, along_y, bottom, coriolis):
        def north_of(values):
            return pltpu.roll(values, ext - 1, 0)

        def south_of(values):
            return pltpu.roll(values, 1, 0)

        wide = thick + turn(thick, -1)
        flux = wide * along_x
        flux_y = (thick + north_of(thick)) * along_y
        vort = (turn(along_y, -1) - along_y) - (north_of(along_x) - along_x) + coriolis
        spin = vort / (wide + north_of(wide))
        turn_y = spin * (flux_y + turn(flux_y, -1))
        turn_x = spin * (flux + north_of(flux))
        square = along_x * along_x
        square_y = along_y * along_y
        total = thick
        for shift in (16, 32, 64):
            total = total + turn(total, shift)
        bern = 0.5 * ((square + turn(square, 1)) + (square_y + south_of(square_y))) + (bottom + total) + weight * thick
        rate_h = -((flux - turn(flux, 1)) + (flux_y - south_of(flux_y)))
        rate_u = (south_of(turn_y) + turn_y) - (turn(bern, -1) - bern)
        rate_v = -(turn(turn_x, 1) + turn_x) - (north_of(bern) - bern)
        return rate_h, rate_u, rate_v

    rates = strip_rates(*fields)
    middle = []
    for item in range(3):
        value = fields[item] + 0.5 * time_step * rates[item]
        middle.append(jnp.where(closed if item == 1 else outside, 0.0, value))
    rates = strip_rates(*middle, fields[3], fields[4])
    for item in range(3):
        value = 0.5 * (fields[item] + middle[item]) + 0.25 * time_step * rates[item]
        if item == 1:
            value = jnp.where(closed, 0.0, value)
        strip_mid[item] = jnp.where(wide_place < 8, turn(value, -6), turn(value, 6))

    def merge(block, _):
        base = pl.multiple_of(block * SUB, SUB)
        after = pl.multiple_of(block * SUB + SUB, SUB)
        for item in range(3):
            value = strip_mid[item, pl.ds(after, SUB), :]
            for lev in range(levels):
                moved = turn(value, -(GROUP * lev + 8))
                low = result[item, 0, lev, pl.ds(base, SUB), :]
                high = result[item, 1, lev, pl.ds(base, SUB), :]
                result[item, 0, lev, pl.ds(base, SUB), :] = jnp.where(lane < 2, moved, low)
                result[item, 1, lev, pl.ds(base, SUB), :] = jnp.where(lane >= LANES - 4, moved, high)
        return 0

    lax.fori_loop(0, blocks, merge, 0)

    stores = []
    for half in range(2):
        cols = pl.ds(half * LANES, LANES)
        targets = [h_out.at[:, :, cols], vel_out.at[0, :, :, cols], vel_out.at[1, :, :, cols]]
        for item in range(3):
            stores.append(pltpu.make_async_copy(result.at[item, half], targets[item], store_sem.at[half, item]))
    for copy in stores:
        copy.start()
    for copy in along_y:
        copy.wait_send()

    @pl.when(east_open)
    def _():
        for copy in to_east:
            copy.wait_send()

    @pl.when(west_open)
    def _():
        for copy in to_west:
            copy.wait_send()

    for copy in stores:
        copy.wait()


def solution(mesh):
    count_x, count_y = mesh.shape["gx"], mesh.shape["gy"]

    def body(thickness, velocity, bottom, coriolis, reduced):
        levels, rows, columns = thickness.shape
        assert levels == SUB and columns == 2 * LANES and rows % SUB == 0
        ext = rows + 2 * SUB
        f32 = jnp.float32

        def run(*refs):
            kernel(count_x, count_y, rows, *refs)

        anywhere = pl.BlockSpec(memory_space=pl.ANY)
        return pl.pallas_call(
            run,
            out_shape=(
                jax.ShapeDtypeStruct(thickness.shape, f32),
                jax.ShapeDtypeStruct(velocity.shape, f32),
            ),
            in_specs=[anywhere] * 4 + [pl.BlockSpec(memory_space=pltpu.SMEM)],
            out_specs=(anywhere, anywhere),
            scratch_shapes=[
                pltpu.VMEM((3, 2, levels, rows, LANES), f32),
                pltpu.VMEM((3, 2, rows + 2, levels, LANES), f32),
                pltpu.VMEM((3, 2, levels, rows, LANES), f32),
                pltpu.VMEM((2, 3, 2, 2, levels, LANES), f32),
                pltpu.VMEM((2, 3, 2, 2, levels, LANES), f32),
                pltpu.VMEM((2, 2, ext, LANES), f32),
                pltpu.VMEM((5, ext, LANES), f32),
                pltpu.VMEM((3, ext, LANES), f32),
                pltpu.VMEM((2, rows, LANES), f32),
                pltpu.VMEM((ext, LANES), f32),
                pltpu.VMEM((ext, LANES), f32),
                pltpu.SemaphoreType.DMA((2, 5)),
                pltpu.SemaphoreType.DMA((2, 3)),
                pltpu.SemaphoreType.DMA((12,)),
                pltpu.SemaphoreType.DMA((12,)),
            ],
            compiler_params=pltpu.CompilerParams(
                collective_id=0, has_side_effects=True, vmem_limit_bytes=32 * 1024 * 1024
            ),
            cost_estimate=pl.CostEstimate(
                flops=200 * thickness.size, bytes_accessed=28 * thickness.size, transcendentals=0
            ),
        )(thickness, velocity, bottom, coriolis, reduced)

    return jax.shard_map(
        body,
        mesh=mesh,
        in_specs=(P(None, "gy", "gx"), P(None, None, "gy", "gx"), P("gy", "gx"), P("gy", "gx"), P()),
        out_specs=(P(None, "gy", "gx"), P(None, None, "gy", "gx")),
        check_vma=False,
    )
```

```python
import jax
import jax.numpy as jnp
from jax import lax
from jax.experimental import pallas as pl
from jax.experimental.pallas import tpu as pltpu
from jax.sharding import PartitionSpec as P

time_step = 0.1
LANES = 128
SUB = 8
GROUP = 16
UNROLL = 10
MESH = pl.DeviceIdType.MESH


def kernel(
    count_x, count_y, rows,
    h_in, vel_in, bottom_in, coriolis_in, reduced_in,
    h_out, vel_out,
    own, mid, result, edge_send, edge_recv, fixed, strip, strip_mid, pack, west_pack, east_pack,
    reduced_local, load_sem, store_sem, small_sem, send_sem, recv_sem,
):
    levels = SUB
    blocks = rows // SUB
    ext = rows + 2 * SUB
    me_x = lax.axis_index("gx")
    me_y = lax.axis_index("gy")
    west_open = me_x > 0
    east_open = me_x < count_x - 1
    north = lax.rem(me_y + 1, count_y)
    south = lax.rem(me_y + count_y - 1, count_y)

    loads = []
    for half in range(2):
        cols = pl.ds(half * LANES, LANES)
        sources = [h_in.at[:, :, cols], vel_in.at[0, :, :, cols], vel_in.at[1, :, :, cols]]
        for item in range(3):
            loads.append(pltpu.make_async_copy(sources[item], own.at[item, half], load_sem.at[half, item]))
        for item, source in enumerate((bottom_in, coriolis_in)):
            loads.append(
                pltpu.make_async_copy(
                    source.at[:, cols], fixed.at[item, half, pl.ds(SUB, rows)], load_sem.at[half, 3 + item]
                )
            )
    loads.append(pltpu.make_async_copy(reduced_in, reduced_local, small_sem))
    for copy in loads:
        copy.start()

    barrier = pltpu.get_barrier_semaphore()

    def greet(x, y):
        pl.semaphore_signal(barrier, inc=1, device_id={"gx": x, "gy": y}, device_id_type=MESH)

    greet(me_x, north)
    greet(me_x, south)

    @pl.when(west_open)
    def _():
        for y in (north, me_y, south):
            greet(me_x - 1, y)

    @pl.when(east_open)
    def _():
        for y in (north, me_y, south):
            greet(me_x + 1, y)

    @pl.when(jnp.logical_not(west_open))
    def _():
        west_pack[...] = jnp.zeros_like(west_pack)

    @pl.when(jnp.logical_not(east_open))
    def _():
        east_pack[...] = jnp.zeros_like(east_pack)

    lane = lax.broadcasted_iota(jnp.int32, (SUB, LANES), 1)
    sub = lax.broadcasted_iota(jnp.int32, (SUB, LANES), 0)
    level = lane // GROUP
    place = lane - level * GROUP
    for copy in loads:
        copy.wait()
    reduced_main = jnp.zeros((SUB, LANES), jnp.float32)
    reduced_strip = jnp.zeros((SUB, LANES), jnp.float32)
    for item in range(levels):
        value = 2.0 * reduced_local[item]
        reduced_main = jnp.where(sub == item, value, reduced_main)
        reduced_strip = jnp.where(level == item, value, reduced_strip)

    def turn(values, shift):
        return pltpu.roll(values, shift % LANES, 1)

    flat = [[own.at[item, half].reshape(levels * rows, LANES) for half in range(2)] for item in range(3)]

    def own_row(item, half, row):
        return flat[item][half][pl.ds(row, levels, stride=rows), :]

    for item in range(3):
        for half in range(2):
            for row in range(2):
                edge_send[0, item, half, row] = own_row(item, half, rows - 2 + row)
                edge_send[1, item, half, row] = own_row(item, half, row)

    wall_last = jnp.logical_and(place == 13, jnp.logical_not(east_open))

    def spread(gathered):
        left = turn(gathered, -6)
        right = turn(gathered, 6)
        return jnp.where(place < 8, left, right)

    def build(block, _):
        base = pl.multiple_of(block * SUB, SUB)
        after = pl.multiple_of(block * SUB + SUB, SUB)
        made = []
        for item in range(3):
            gathered = jnp.zeros((SUB, LANES), jnp.float32)
            for lev in range(levels):
                low = own[item, 0, lev, pl.ds(base, SUB), :]
                high = own[item, 1, lev, pl.ds(base, SUB), :]
                joined = jnp.where(lane < LANES // 2, low, high)
                gathered = jnp.where(level == lev, turn(joined, GROUP * lev + 8), gathered)
            value = spread(gathered)
            if item == 1:
                value = jnp.where(wall_last, 0.0, value)
            made.append(value)
        for item in range(2):
            low = fixed[item, 0, pl.ds(after, SUB), :]
            high = fixed[item, 1, pl.ds(after, SUB), :]
            joined = turn(jnp.where(lane < LANES // 2, low, high), 8)
            gathered = jnp.where(lane < GROUP, joined, 0.0)
            for shift in (16, 32, 64):
                gathered = gathered + turn(gathered, shift)
            made.append(spread(gathered))
        for item in range(5):
            strip[item, pl.ds(after, SUB), :] = made[item]
        eastbound = turn(made[4], -4)
        westbound = turn(made[4], 4)
        for item in (3, 2, 1, 0):
            eastbound = jnp.where(place < 2 * item + 2, turn(made[item], 2 * item - 12), eastbound)
            westbound = jnp.where(place >= 14 - 2 * item, turn(made[item], 12 - 2 * item), westbound)
        pack[0, pl.ds(base, SUB), :] = eastbound
        pack[1, pl.ds(base, SUB), :] = westbound
        return 0

    lax.fori_loop(0, blocks, build, 0)

    first = pl.ds(0, SUB)
    last = pl.ds(rows - SUB, SUB)
    own_first = pl.ds(SUB, SUB)
    own_last = pl.ds(rows, SUB)
    ext_last = pl.ds(rows + SUB, SUB)
    ext_own = pl.ds(SUB, rows)

    def remote(index, source, target, x, y):
        return pltpu.make_async_remote_copy(
            src_ref=source,
            dst_ref=target,
            send_sem=send_sem.at[index],
            recv_sem=recv_sem.at[index],
            device_id={"gx": x, "gy": y},
            device_id_type=MESH,
        )

    along_y = [
        remote(0, edge_send.at[0], edge_recv.at[0], me_x, north),
        remote(1, edge_send.at[1], edge_recv.at[1], me_x, south),
        remote(2, fixed.at[:, :, own_last], fixed.at[:, :, first], me_x, north),
        remote(3, fixed.at[:, :, own_first], fixed.at[:, :, ext_last], me_x, south),
        remote(4, strip.at[:, own_last], strip.at[:, first], me_x, north),
        remote(5, strip.at[:, own_first], strip.at[:, ext_last], me_x, south),
    ]
    to_east = [
        remote(6, pack.at[0], west_pack.at[ext_own], me_x + 1, me_y),
        remote(7, pack.at[0, last], west_pack.at[first], me_x + 1, north),
        remote(8, pack.at[0, first], west_pack.at[ext_last], me_x + 1, south),
    ]
    to_west = [
        remote(9, pack.at[1], east_pack.at[ext_own], me_x - 1, me_y),
        remote(10, pack.at[1, last], east_pack.at[first], me_x - 1, north),
        remote(11, pack.at[1, first], east_pack.at[ext_last], me_x - 1, south),
    ]

    greeted = 2 + 3 * west_open.astype(jnp.int32) + 3 * east_open.astype(jnp.int32)
    pl.semaphore_wait(barrier, greeted)
    for copy in along_y:
        copy.start()

    @pl.when(east_open)
    def _():
        for copy in to_east:
            copy.start()

    @pl.when(west_open)
    def _():
        for copy in to_west:
            copy.start()

    before_end = lane < LANES - 1
    at_start = lane == 0

    def eastward(pair):
        low, high = turn(pair[0], -1), turn(pair[1], -1)
        return [jnp.where(before_end, low, high), high]

    def westward(pair):
        low, high = turn(pair[0], 1), turn(pair[1], 1)
        return [low, jnp.where(at_start, low, high)]

    def each(function, *pairs):
        return [function(*items) for items in zip(*pairs)]

    def begin(row):
        thick, along_x, along_y = row
        wide = each(lambda a, b: a + b, thick, eastward(thick))
        flux = each(lambda a, b: a * b, wide, along_x)
        zero = [jnp.zeros((SUB, LANES), jnp.float32)] * 2
        return [thick, along_x, along_y, wide, flux, zero, zero, zero]

    def advance(carry, following, bottom_next, coriolis):
        thick, along_x, along_y, wide, flux, bern, flux_y_before, turn_before = carry
        thick_n, along_x_n, along_y_n = following
        wide_n = each(lambda a, b: a + b, thick_n, eastward(thick_n))
        flux_n = each(lambda a, b: a * b, wide_n, along_x_n)
        flux_y = each(lambda a, b, c: (a + b) * c, thick, thick_n, along_y)
        vort = each(
            lambda e, v, un, u, f: (e - v) - (un - u) + f,
            eastward(along_y), along_y, along_x_n, along_x, coriolis,
        )
        spin = each(lambda z, a, b: z / (a + b), vort, wide, wide_n)
        turn_y = each(lambda w, a, b: w * (a + b), spin, flux_y, eastward(flux_y))
        turn_x = each(lambda w, a, b: w * (a + b), spin, flux, flux_n)
        square = each(lambda a: a * a, along_x_n)
        bern_n = each(
            lambda s, w, vn, v, b, h: 0.5 * ((s + w) + (vn * vn + v * v))
            + (b + jnp.sum(h, axis=0, keepdims=True))
            + reduced_main * h,
            square, westward(square), along_y_n, along_y, bottom_next, thick_n,
        )
        rate_h = each(
            lambda f, w, g, p: -((f - w) + (g - p)), flux, westward(flux), flux_y, flux_y_before
        )
        rate_u = each(lambda p, t, e, b: (p + t) - (e - b), turn_before, turn_y, eastward(bern), bern)
        rate_v = each(lambda w, t, n, b: -(w + t) - (n - b), westward(turn_x), turn_x, bern_n, bern)
        carry = [thick_n, along_x_n, along_y_n, wide_n, flux_n, bern_n, flux_y, turn_y]
        return carry, [rate_h, rate_u, rate_v]

    def fixed_row(item, row):
        return [
            jnp.broadcast_to(fixed[item, half, pl.ds(row + SUB, 1), :], (SUB, LANES)) for half in range(2)
        ]

    def start_row(row):
        return [[own_row(item, half, row) for half in range(2)] for item in range(3)]

    def halo_row(side, row):
        return [[edge_recv[side, item, half, row] for half in range(2)] for item in range(3)]

    def mid_row(row):
        return [[mid[item, half, row + 1] for half in range(2)] for item in range(3)]

    def keep_mid(row, carry, rates):
        for item in range(3):
            for half in range(2):
                mid[item, half, row + 1] = carry[item][half] + 0.5 * time_step * rates[item][half]

    def first_step(carry, row, following):
        after, rates = advance(carry, following, fixed_row(0, row + 1), fixed_row(1, row))
        keep_mid(row, carry, rates)
        return after

    def sweep(carry, start, stop, step):
        whole = (stop - start) // UNROLL

        def some(block, carry):
            for extra in range(UNROLL):
                carry = step(carry, start + block * UNROLL + extra)
            return carry

        carry = lax.fori_loop(0, whole, some, carry)
        for row in range(start + whole * UNROLL, stop):
            carry = step(carry, row)
        return carry

    carry = begin(start_row(0))
    carry, _ = advance(carry, start_row(1), fixed_row(0, 1), fixed_row(1, 0))
    sweep(carry, 1, rows - 1, lambda carry, row: first_step(carry, row, start_row(row + 1)))

    out_flat = [[result.at[item, half].reshape(levels * rows, LANES) for half in range(2)] for item in range(3)]

    def second_step(carry, row):
        after, rates = advance(carry, mid_row(row + 1), fixed_row(0, row + 1), fixed_row(1, row))
        start = start_row(row)
        for item in range(3):
            for half in range(2):
                value = 0.5 * (start[item][half] + carry[item][half]) + 0.25 * time_step * rates[item][half]
                out_flat[item][half][pl.ds(row, levels, stride=rows), :] = value
        return after

    def second_sweep(start, stop):
        carry = begin(mid_row(start - 1))
        carry, _ = advance(carry, mid_row(start), fixed_row(0, start), fixed_row(1, start - 1))
        sweep(carry, start, stop, second_step)

    second_sweep(2, rows - 2)

    for copy in along_y[:4]:
        copy.wait_recv()
    south_rows = [halo_row(0, 0), halo_row(0, 1), start_row(0), start_row(1)]
    carry = begin(south_rows[0])
    carry, _ = advance(carry, south_rows[1], fixed_row(0, -1), fixed_row(1, -2))
    for row in (-1, 0):
        carry = first_step(carry, row, south_rows[row + 3])
    north_rows = [start_row(rows - 2), start_row(rows - 1), halo_row(1, 0), halo_row(1, 1)]
    carry = begin(north_rows[0])
    carry, _ = advance(carry, north_rows[1], fixed_row(0, rows - 1), fixed_row(1, rows - 2))
    for step in range(2):
        carry = first_step(carry, rows - 1 + step, north_rows[step + 2])
    second_sweep(0, 2)
    second_sweep(rows - 2, rows)

    for copy in along_y[4:]:
        copy.wait_recv()

    @pl.when(west_open)
    def _():
        for copy in to_east:
            copy.wait_recv()

    @pl.when(east_open)
    def _():
        for copy in to_west:
            copy.wait_recv()

    wide_lane = lax.broadcasted_iota(jnp.int32, (ext, LANES), 1)
    wide_place = wide_lane - (wide_lane // GROUP) * GROUP
    from_west = wide_place < 2
    from_east = wide_place >= 14
    outside = jnp.logical_or(
        jnp.logical_and(from_west, jnp.logical_not(west_open)),
        jnp.logical_and(from_east, jnp.logical_not(east_open)),
    )
    closed = jnp.logical_or(outside, jnp.logical_and(wide_place == 13, jnp.logical_not(east_open)))
    received_west = west_pack[...]
    received_east = east_pack[...]
    fields = []
    for item in range(5):
        value = jnp.where(from_west, turn(received_west, -2 * item), strip[item])
        fields.append(jnp.where(from_east, turn(received_east, 2 * item), value))
    weight = jnp.concatenate([reduced_strip] * (ext // SUB), axis=0)

    def strip_rates(thick, along_x, along_y, bottom, coriolis):
        def north_of(values):
            return pltpu.roll(values, ext - 1, 0)

        def south_of(values):
            return pltpu.roll(values, 1, 0)

        wide = thick + turn(thick, -1)
        flux = wide * along_x
        flux_y = (thick + north_of(thick)) * along_y
        vort = (turn(along_y, -1) - along_y) - (north_of(along_x) - along_x) + coriolis
        spin = vort / (wide + north_of(wide))
        turn_y = spin * (flux_y + turn(flux_y, -1))
        turn_x = spin * (flux + north_of(flux))
        square = along_x * along_x
        square_y = along_y * along_y
        total = thick
        for shift in (16, 32, 64):
            total = total + turn(total, shift)
        bern = 0.5 * ((square + turn(square, 1)) + (square_y + south_of(square_y))) + (bottom + total) + weight * thick
        rate_h = -((flux - turn(flux, 1)) + (flux_y - south_of(flux_y)))
        rate_u = (south_of(turn_y) + turn_y) - (turn(bern, -1) - bern)
        rate_v = -(turn(turn_x, 1) + turn_x) - (north_of(bern) - bern)
        return rate_h, rate_u, rate_v

    rates = strip_rates(*fields)
    middle = []
    for item in range(3):
        value = fields[item] + 0.5 * time_step * rates[item]
        middle.append(jnp.where(closed if item == 1 else outside, 0.0, value))
    rates = strip_rates(*middle, fields[3], fields[4])
    for item in range(3):
        value = 0.5 * (fields[item] + middle[item]) + 0.25 * time_step * rates[item]
        if item == 1:
            value = jnp.where(closed, 0.0, value)
        strip_mid[item] = jnp.where(wide_place < 8, turn(value, -6), turn(value, 6))

    def merge(block, _):
        base = pl.multiple_of(block * SUB, SUB)
        after = pl.multiple_of(block * SUB + SUB, SUB)
        for item in range(3):
            value = strip_mid[item, pl.ds(after, SUB), :]
            for lev in range(levels):
                moved = turn(value, -(GROUP * lev + 8))
                low = result[item, 0, lev, pl.ds(base, SUB), :]
                high = result[item, 1, lev, pl.ds(base, SUB), :]
                result[item, 0, lev, pl.ds(base, SUB), :] = jnp.where(lane < 2, moved, low)
                result[item, 1, lev, pl.ds(base, SUB), :] = jnp.where(lane >= LANES - 4, moved, high)
        return 0

    stores = []
    half_blocks = (blocks + 1) // 2
    for group, (start, stop) in enumerate(((0, half_blocks), (half_blocks, blocks))):
        lax.fori_loop(start, stop, merge, 0)
        part = pl.ds(start * SUB, (stop - start) * SUB)
        for half in range(2):
            cols = pl.ds(half * LANES, LANES)
            targets = [h_out.at[:, part, cols], vel_out.at[0, :, part, cols], vel_out.at[1, :, part, cols]]
            for item in range(3):
                copy = pltpu.make_async_copy(
                    result.at[item, half, :, part], targets[item], store_sem.at[group, half, item]
                )
                copy.start()
                stores.append(copy)
    for copy in along_y:
        copy.wait_send()

    @pl.when(east_open)
    def _():
        for copy in to_east:
            copy.wait_send()

    @pl.when(west_open)
    def _():
        for copy in to_west:
            copy.wait_send()

    for copy in stores:
        copy.wait()


def solution(mesh):
    count_x, count_y = mesh.shape["gx"], mesh.shape["gy"]

    def body(thickness, velocity, bottom, coriolis, reduced):
        levels, rows, columns = thickness.shape
        assert levels == SUB and columns == 2 * LANES and rows % SUB == 0
        ext = rows + 2 * SUB
        f32 = jnp.float32

        def run(*refs):
            kernel(count_x, count_y, rows, *refs)

        in_hbm = pl.BlockSpec(memory_space=pltpu.HBM)
        return pl.pallas_call(
            run,
            out_shape=(
                jax.ShapeDtypeStruct(thickness.shape, f32),
                jax.ShapeDtypeStruct(velocity.shape, f32),
            ),
            in_specs=[in_hbm] * 5,
            out_specs=(in_hbm, in_hbm),
            scratch_shapes=[
                pltpu.VMEM((3, 2, levels, rows, LANES), f32),
                pltpu.VMEM((3, 2, rows + 2, levels, LANES), f32),
                pltpu.VMEM((3, 2, levels, rows, LANES), f32),
                pltpu.VMEM((2, 3, 2, 2, levels, LANES), f32),
                pltpu.VMEM((2, 3, 2, 2, levels, LANES), f32),
                pltpu.VMEM((2, 2, ext, LANES), f32),
                pltpu.VMEM((5, ext, LANES), f32),
                pltpu.VMEM((3, ext, LANES), f32),
                pltpu.VMEM((2, rows, LANES), f32),
                pltpu.VMEM((ext, LANES), f32),
                pltpu.VMEM((ext, LANES), f32),
                pltpu.SMEM((levels,), f32),
                pltpu.SemaphoreType.DMA((2, 5)),
                pltpu.SemaphoreType.DMA((2, 2, 3)),
                pltpu.SemaphoreType.DMA,
                pltpu.SemaphoreType.DMA((12,)),
                pltpu.SemaphoreType.DMA((12,)),
            ],
            compiler_params=pltpu.CompilerParams(
                collective_id=0, has_side_effects=True, vmem_limit_bytes=62 * 1024 * 1024
            ),
            cost_estimate=pl.CostEstimate(
                flops=200 * thickness.size, bytes_accessed=28 * thickness.size, transcendentals=0
            ),
        )(thickness, velocity, bottom, coriolis, reduced)

    return jax.shard_map(
        body,
        mesh=mesh,
        in_specs=(P(None, "gy", "gx"), P(None, None, "gy", "gx"), P("gy", "gx"), P("gy", "gx"), P()),
        out_specs=(P(None, "gy", "gx"), P(None, None, "gy", "gx")),
        check_vma=False,
    )
```

```python
import jax
import jax.numpy as jnp
from jax import lax
from jax.experimental import pallas as pl
from jax.experimental.pallas import tpu as pltpu
from jax.sharding import PartitionSpec as P

time_step = 0.1
LANES = 128
SUB = 8
GROUP = 16
UNROLL = 10
VMEM_MAIN = 58 * 1024 * 1024
VMEM_END = 16 * 1024 * 1024
MESH = pl.DeviceIdType.MESH


def kernel(
    count_x, count_y, rows,
    h_in, vel_in, bottom_in, coriolis_in, reduced_in,
    result, strip_out,
    own, mid, edge_send, edge_recv, fixed, strip, pack, west_pack, east_pack,
    reduced_local, load_sem, small_sem, send_sem, recv_sem,
):
    levels = SUB
    blocks = rows // SUB
    ext = rows + 2 * SUB
    me_x = lax.axis_index("gx")
    me_y = lax.axis_index("gy")
    west_open = me_x > 0
    east_open = me_x < count_x - 1
    north = lax.rem(me_y + 1, count_y)
    south = lax.rem(me_y + count_y - 1, count_y)

    loads = []
    for half in range(2):
        cols = pl.ds(half * LANES, LANES)
        sources = [h_in.at[:, :, cols], vel_in.at[0, :, :, cols], vel_in.at[1, :, :, cols]]
        for item in range(3):
            loads.append(pltpu.make_async_copy(sources[item], own.at[item, half], load_sem.at[half, item]))
        for item, source in enumerate((bottom_in, coriolis_in)):
            loads.append(
                pltpu.make_async_copy(
                    source.at[:, cols], fixed.at[item, half, pl.ds(SUB, rows)], load_sem.at[half, 3 + item]
                )
            )
    loads.append(pltpu.make_async_copy(reduced_in, reduced_local, small_sem))
    for copy in loads:
        copy.start()

    barrier = pltpu.get_barrier_semaphore()

    def greet(x, y):
        pl.semaphore_signal(barrier, inc=1, device_id={"gx": x, "gy": y}, device_id_type=MESH)

    greet(me_x, north)
    greet(me_x, south)

    @pl.when(west_open)
    def _():
        for y in (north, me_y, south):
            greet(me_x - 1, y)

    @pl.when(east_open)
    def _():
        for y in (north, me_y, south):
            greet(me_x + 1, y)

    @pl.when(jnp.logical_not(west_open))
    def _():
        west_pack[...] = jnp.zeros_like(west_pack)

    @pl.when(jnp.logical_not(east_open))
    def _():
        east_pack[...] = jnp.zeros_like(east_pack)

    lane = lax.broadcasted_iota(jnp.int32, (SUB, LANES), 1)
    sub = lax.broadcasted_iota(jnp.int32, (SUB, LANES), 0)
    level = lane // GROUP
    place = lane - level * GROUP
    for copy in loads:
        copy.wait()
    reduced_main = jnp.zeros((SUB, LANES), jnp.float32)
    reduced_strip = jnp.zeros((SUB, LANES), jnp.float32)
    for item in range(levels):
        value = 2.0 * reduced_local[item]
        reduced_main = jnp.where(sub == item, value, reduced_main)
        reduced_strip = jnp.where(level == item, value, reduced_strip)

    def turn(values, shift):
        return pltpu.roll(values, shift % LANES, 1)

    flat = [[own.at[item, half].reshape(levels * rows, LANES) for half in range(2)] for item in range(3)]

    def own_row(item, half, row):
        return flat[item][half][pl.ds(row, levels, stride=rows), :]

    for item in range(3):
        for half in range(2):
            for row in range(2):
                edge_send[0, item, half, row] = own_row(item, half, rows - 2 + row)
                edge_send[1, item, half, row] = own_row(item, half, row)

    wall_last = jnp.logical_and(place == 13, jnp.logical_not(east_open))

    def spread(gathered):
        left = turn(gathered, -6)
        right = turn(gathered, 6)
        return jnp.where(place < 8, left, right)

    def build(block, _):
        base = pl.multiple_of(block * SUB, SUB)
        after = pl.multiple_of(block * SUB + SUB, SUB)
        made = []
        for item in range(3):
            gathered = jnp.zeros((SUB, LANES), jnp.float32)
            for lev in range(levels):
                low = own[item, 0, lev, pl.ds(base, SUB), :]
                high = own[item, 1, lev, pl.ds(base, SUB), :]
                joined = jnp.where(lane < LANES // 2, low, high)
                gathered = jnp.where(level == lev, turn(joined, GROUP * lev + 8), gathered)
            value = spread(gathered)
            if item == 1:
                value = jnp.where(wall_last, 0.0, value)
            made.append(value)
        for item in range(2):
            low = fixed[item, 0, pl.ds(after, SUB), :]
            high = fixed[item, 1, pl.ds(after, SUB), :]
            joined = turn(jnp.where(lane < LANES // 2, low, high), 8)
            gathered = jnp.where(lane < GROUP, joined, 0.0)
            for shift in (16, 32, 64):
                gathered = gathered + turn(gathered, shift)
            made.append(spread(gathered))
        for item in range(5):
            strip[item, pl.ds(after, SUB), :] = made[item]
        eastbound = turn(made[4], -4)
        westbound = turn(made[4], 4)
        for item in (3, 2, 1, 0):
            eastbound = jnp.where(place < 2 * item + 2, turn(made[item], 2 * item - 12), eastbound)
            westbound = jnp.where(place >= 14 - 2 * item, turn(made[item], 12 - 2 * item), westbound)
        pack[0, pl.ds(base, SUB), :] = eastbound
        pack[1, pl.ds(base, SUB), :] = westbound
        return 0

    lax.fori_loop(0, blocks, build, 0)

    first = pl.ds(0, SUB)
    last = pl.ds(rows - SUB, SUB)
    own_first = pl.ds(SUB, SUB)
    own_last = pl.ds(rows, SUB)
    ext_last = pl.ds(rows + SUB, SUB)
    ext_own = pl.ds(SUB, rows)

    def remote(index, source, target, x, y):
        return pltpu.make_async_remote_copy(
            src_ref=source,
            dst_ref=target,
            send_sem=send_sem.at[index],
            recv_sem=recv_sem.at[index],
            device_id={"gx": x, "gy": y},
            device_id_type=MESH,
        )

    along_y = [
        remote(0, edge_send.at[0], edge_recv.at[0], me_x, north),
        remote(1, edge_send.at[1], edge_recv.at[1], me_x, south),
        remote(2, fixed.at[:, :, own_last], fixed.at[:, :, first], me_x, north),
        remote(3, fixed.at[:, :, own_first], fixed.at[:, :, ext_last], me_x, south),
        remote(4, strip.at[:, own_last], strip.at[:, first], me_x, north),
        remote(5, strip.at[:, own_first], strip.at[:, ext_last], me_x, south),
    ]
    to_east = [
        remote(6, pack.at[0], west_pack.at[ext_own], me_x + 1, me_y),
        remote(7, pack.at[0, last], west_pack.at[first], me_x + 1, north),
        remote(8, pack.at[0, first], west_pack.at[ext_last], me_x + 1, south),
    ]
    to_west = [
        remote(9, pack.at[1], east_pack.at[ext_own], me_x - 1, me_y),
        remote(10, pack.at[1, last], east_pack.at[first], me_x - 1, north),
        remote(11, pack.at[1, first], east_pack.at[ext_last], me_x - 1, south),
    ]

    greeted = 2 + 3 * west_open.astype(jnp.int32) + 3 * east_open.astype(jnp.int32)
    pl.semaphore_wait(barrier, greeted)
    for copy in along_y:
        copy.start()

    @pl.when(east_open)
    def _():
        for copy in to_east:
            copy.start()

    @pl.when(west_open)
    def _():
        for copy in to_west:
            copy.start()

    before_end = lane < LANES - 1
    at_start = lane == 0

    def eastward(pair):
        low, high = turn(pair[0], -1), turn(pair[1], -1)
        return [jnp.where(before_end, low, high), high]

    def westward(pair):
        low, high = turn(pair[0], 1), turn(pair[1], 1)
        return [low, jnp.where(at_start, low, high)]

    def each(function, *pairs):
        return [function(*items) for items in zip(*pairs)]

    def begin(row):
        thick, along_x, along_y = row
        wide = each(lambda a, b: a + b, thick, eastward(thick))
        flux = each(lambda a, b: a * b, wide, along_x)
        zero = [jnp.zeros((SUB, LANES), jnp.float32)] * 2
        return [thick, along_x, along_y, wide, flux, zero, zero, zero]

    def advance(carry, following, bottom_next, coriolis):
        thick, along_x, along_y, wide, flux, bern, flux_y_before, turn_before = carry
        thick_n, along_x_n, along_y_n = following
        wide_n = each(lambda a, b: a + b, thick_n, eastward(thick_n))
        flux_n = each(lambda a, b: a * b, wide_n, along_x_n)
        flux_y = each(lambda a, b, c: (a + b) * c, thick, thick_n, along_y)
        vort = each(
            lambda e, v, un, u, f: (e - v) - (un - u) + f,
            eastward(along_y), along_y, along_x_n, along_x, coriolis,
        )
        spin = each(lambda z, a, b: z / (a + b), vort, wide, wide_n)
        turn_y = each(lambda w, a, b: w * (a + b), spin, flux_y, eastward(flux_y))
        turn_x = each(lambda w, a, b: w * (a + b), spin, flux, flux_n)
        square = each(lambda a: a * a, along_x_n)
        bern_n = each(
            lambda s, w, vn, v, b, h: 0.5 * ((s + w) + (vn * vn + v * v))
            + (b + jnp.sum(h, axis=0, keepdims=True))
            + reduced_main * h,
            square, westward(square), along_y_n, along_y, bottom_next, thick_n,
        )
        rate_h = each(
            lambda f, w, g, p: -((f - w) + (g - p)), flux, westward(flux), flux_y, flux_y_before
        )
        rate_u = each(lambda p, t, e, b: (p + t) - (e - b), turn_before, turn_y, eastward(bern), bern)
        rate_v = each(lambda w, t, n, b: -(w + t) - (n - b), westward(turn_x), turn_x, bern_n, bern)
        carry = [thick_n, along_x_n, along_y_n, wide_n, flux_n, bern_n, flux_y, turn_y]
        return carry, [rate_h, rate_u, rate_v]

    def fixed_row(item, row):
        return [
            jnp.broadcast_to(fixed[item, half, pl.ds(row + SUB, 1), :], (SUB, LANES)) for half in range(2)
        ]

    def start_row(row):
        return [[own_row(item, half, row) for half in range(2)] for item in range(3)]

    def halo_row(side, row):
        return [[edge_recv[side, item, half, row] for half in range(2)] for item in range(3)]

    def mid_row(row):
        return [[mid[item, half, row + 1] for half in range(2)] for item in range(3)]

    def keep_mid(row, carry, rates):
        for item in range(3):
            for half in range(2):
                mid[item, half, row + 1] = carry[item][half] + 0.5 * time_step * rates[item][half]

    def first_step(carry, row, following):
        after, rates = advance(carry, following, fixed_row(0, row + 1), fixed_row(1, row))
        keep_mid(row, carry, rates)
        return after

    def sweep(carry, start, stop, step):
        whole = (stop - start) // UNROLL

        def some(block, carry):
            for extra in range(UNROLL):
                carry = step(carry, start + block * UNROLL + extra)
            return carry

        carry = lax.fori_loop(0, whole, some, carry)
        for row in range(start + whole * UNROLL, stop):
            carry = step(carry, row)
        return carry

    carry = begin(start_row(0))
    carry, _ = advance(carry, start_row(1), fixed_row(0, 1), fixed_row(1, 0))
    sweep(carry, 1, rows - 1, lambda carry, row: first_step(carry, row, start_row(row + 1)))

    out_flat = [[result.at[item, half].reshape(levels * rows, LANES) for half in range(2)] for item in range(3)]

    def second_step(carry, row):
        after, rates = advance(carry, mid_row(row + 1), fixed_row(0, row + 1), fixed_row(1, row))
        start = start_row(row)
        for item in range(3):
            for half in range(2):
                value = 0.5 * (start[item][half] + carry[item][half]) + 0.25 * time_step * rates[item][half]
                out_flat[item][half][pl.ds(row, levels, stride=rows), :] = value
        return after

    def second_sweep(start, stop):
        carry = begin(mid_row(start - 1))
        carry, _ = advance(carry, mid_row(start), fixed_row(0, start), fixed_row(1, start - 1))
        sweep(carry, start, stop, second_step)

    second_sweep(2, rows - 2)

    for copy in along_y[:4]:
        copy.wait_recv()
    south_rows = [halo_row(0, 0), halo_row(0, 1), start_row(0), start_row(1)]
    carry = begin(south_rows[0])
    carry, _ = advance(carry, south_rows[1], fixed_row(0, -1), fixed_row(1, -2))
    for row in (-1, 0):
        carry = first_step(carry, row, south_rows[row + 3])
    north_rows = [start_row(rows - 2), start_row(rows - 1), halo_row(1, 0), halo_row(1, 1)]
    carry = begin(north_rows[0])
    carry, _ = advance(carry, north_rows[1], fixed_row(0, rows - 1), fixed_row(1, rows - 2))
    for step in range(2):
        carry = first_step(carry, rows - 1 + step, north_rows[step + 2])
    second_sweep(0, 2)
    second_sweep(rows - 2, rows)

    for copy in along_y[4:]:
        copy.wait_recv()

    @pl.when(west_open)
    def _():
        for copy in to_east:
            copy.wait_recv()

    @pl.when(east_open)
    def _():
        for copy in to_west:
            copy.wait_recv()

    wide_lane = lax.broadcasted_iota(jnp.int32, (ext, LANES), 1)
    wide_place = wide_lane - (wide_lane // GROUP) * GROUP
    from_west = wide_place < 2
    from_east = wide_place >= 14
    outside = jnp.logical_or(
        jnp.logical_and(from_west, jnp.logical_not(west_open)),
        jnp.logical_and(from_east, jnp.logical_not(east_open)),
    )
    closed = jnp.logical_or(outside, jnp.logical_and(wide_place == 13, jnp.logical_not(east_open)))
    received_west = west_pack[...]
    received_east = east_pack[...]
    fields = []
    for item in range(5):
        value = jnp.where(from_west, turn(received_west, -2 * item), strip[item])
        fields.append(jnp.where(from_east, turn(received_east, 2 * item), value))
    weight = jnp.concatenate([reduced_strip] * (ext // SUB), axis=0)

    def strip_rates(thick, along_x, along_y, bottom, coriolis):
        def north_of(values):
            return pltpu.roll(values, ext - 1, 0)

        def south_of(values):
            return pltpu.roll(values, 1, 0)

        wide = thick + turn(thick, -1)
        flux = wide * along_x
        flux_y = (thick + north_of(thick)) * along_y
        vort = (turn(along_y, -1) - along_y) - (north_of(along_x) - along_x) + coriolis
        spin = vort / (wide + north_of(wide))
        turn_y = spin * (flux_y + turn(flux_y, -1))
        turn_x = spin * (flux + north_of(flux))
        square = along_x * along_x
        square_y = along_y * along_y
        total = thick
        for shift in (16, 32, 64):
            total = total + turn(total, shift)
        bern = 0.5 * ((square + turn(square, 1)) + (square_y + south_of(square_y))) + (bottom + total) + weight * thick
        rate_h = -((flux - turn(flux, 1)) + (flux_y - south_of(flux_y)))
        rate_u = (south_of(turn_y) + turn_y) - (turn(bern, -1) - bern)
        rate_v = -(turn(turn_x, 1) + turn_x) - (north_of(bern) - bern)
        return rate_h, rate_u, rate_v

    rates = strip_rates(*fields)
    middle = []
    for item in range(3):
        value = fields[item] + 0.5 * time_step * rates[item]
        middle.append(jnp.where(closed if item == 1 else outside, 0.0, value))
    rates = strip_rates(*middle, fields[3], fields[4])
    for item in range(3):
        value = 0.5 * (fields[item] + middle[item]) + 0.25 * time_step * rates[item]
        if item == 1:
            value = jnp.where(closed, 0.0, value)
        strip_out[item] = jnp.where(wide_place < 8, turn(value, -6), turn(value, 6))

    for copy in along_y:
        copy.wait_send()

    @pl.when(east_open)
    def _():
        for copy in to_east:
            copy.wait_send()

    @pl.when(west_open)
    def _():
        for copy in to_west:
            copy.wait_send()


def finish(rows, result, strip_out, h_out, vel_out, merged, store_sem):
    levels = SUB
    blocks = rows // SUB
    lane = lax.broadcasted_iota(jnp.int32, (SUB, LANES), 1)

    stores = []
    for block in range(blocks):
        part = pl.ds(block * SUB, SUB)
        for item in range(3):
            value = strip_out[item, pl.ds(block * SUB + SUB, SUB), :]
            for lev in range(levels):
                moved = pltpu.roll(value, LANES - (GROUP * lev + 8) % LANES, 1)
                low = result[item, 0, lev, part, :]
                high = result[item, 1, lev, part, :]
                merged[item, lev, part, pl.ds(0, LANES)] = jnp.where(lane < 2, moved, low)
                merged[item, lev, part, pl.ds(LANES, LANES)] = jnp.where(lane >= LANES - 4, moved, high)
        targets = [h_out.at[:, part], vel_out.at[0, :, part], vel_out.at[1, :, part]]
        for item in range(3):
            copy = pltpu.make_async_copy(merged.at[item, :, part], targets[item], store_sem.at[block, item])
            copy.start()
            stores.append(copy)
    for copy in stores:
        copy.wait()


def solution(mesh):
    count_x, count_y = mesh.shape["gx"], mesh.shape["gy"]

    def body(thickness, velocity, bottom, coriolis, reduced):
        levels, rows, columns = thickness.shape
        assert levels == SUB and columns == 2 * LANES and rows % SUB == 0
        ext = rows + 2 * SUB
        f32 = jnp.float32

        def run(*refs):
            kernel(count_x, count_y, rows, *refs)

        in_hbm = pl.BlockSpec(memory_space=pltpu.HBM)
        in_vmem = pl.BlockSpec(memory_space=pltpu.VMEM)
        result, strip_out = pl.pallas_call(
            run,
            out_shape=(
                pltpu.VMEM((3, 2, levels, rows, LANES), f32),
                pltpu.VMEM((3, ext, LANES), f32),
            ),
            in_specs=[in_hbm] * 5,
            out_specs=(in_vmem, in_vmem),
            scratch_shapes=[
                pltpu.VMEM((3, 2, levels, rows, LANES), f32),
                pltpu.VMEM((3, 2, rows + 2, levels, LANES), f32),
                pltpu.VMEM((2, 3, 2, 2, levels, LANES), f32),
                pltpu.VMEM((2, 3, 2, 2, levels, LANES), f32),
                pltpu.VMEM((2, 2, ext, LANES), f32),
                pltpu.VMEM((5, ext, LANES), f32),
                pltpu.VMEM((2, rows, LANES), f32),
                pltpu.VMEM((ext, LANES), f32),
                pltpu.VMEM((ext, LANES), f32),
                pltpu.SMEM((levels,), f32),
                pltpu.SemaphoreType.DMA((2, 5)),
                pltpu.SemaphoreType.DMA,
                pltpu.SemaphoreType.DMA((12,)),
                pltpu.SemaphoreType.DMA((12,)),
            ],
            compiler_params=pltpu.CompilerParams(
                collective_id=0, has_side_effects=True, vmem_limit_bytes=VMEM_MAIN
            ),
            cost_estimate=pl.CostEstimate(
                flops=200 * thickness.size, bytes_accessed=28 * thickness.size, transcendentals=0
            ),
        )(thickness, velocity, bottom, coriolis, reduced)

        def end(*refs):
            finish(rows, *refs)

        return pl.pallas_call(
            end,
            out_shape=(
                jax.ShapeDtypeStruct(thickness.shape, f32),
                jax.ShapeDtypeStruct(velocity.shape, f32),
            ),
            in_specs=[in_vmem] * 2,
            out_specs=(in_hbm, in_hbm),
            scratch_shapes=[
                pltpu.VMEM((3, levels, rows, columns), f32),
                pltpu.SemaphoreType.DMA((rows // SUB, 3)),
            ],
            compiler_params=pltpu.CompilerParams(vmem_limit_bytes=VMEM_END),
            cost_estimate=pl.CostEstimate(
                flops=thickness.size, bytes_accessed=24 * thickness.size, transcendentals=0
            ),
        )(result, strip_out)

    return jax.shard_map(
        body,
        mesh=mesh,
        in_specs=(P(None, "gy", "gx"), P(None, None, "gy", "gx"), P("gy", "gx"), P("gy", "gx"), P()),
        out_specs=(P(None, "gy", "gx"), P(None, None, "gy", "gx")),
        check_vma=False,
    )
```

```python
import jax
import jax.numpy as jnp
from jax import lax
from jax.experimental import pallas as pl
from jax.experimental.pallas import tpu as pltpu
from jax.sharding import PartitionSpec as P

time_step = 0.1
LANES = 128
SUB = 8
GROUP = 16
UNROLL = 10
GROUPS = 2
VMEM_MAIN = 58 * 1024 * 1024
VMEM_END = 16 * 1024 * 1024
MESH = pl.DeviceIdType.MESH


def kernel(
    count_x, count_y, rows,
    h_in, vel_in, bottom_in, coriolis_in, reduced_in,
    result, strip_out,
    own, by_row, mid, fixed, strip, pack, west_pack, east_pack,
    reduced_local, load_sem, small_sem, row_sem, send_sem, recv_sem,
):
    levels = SUB
    blocks = rows // SUB
    ext = rows + 2 * SUB
    me_x = lax.axis_index("gx")
    me_y = lax.axis_index("gy")
    west_open = me_x > 0
    east_open = me_x < count_x - 1
    north = lax.rem(me_y + 1, count_y)
    south = lax.rem(me_y + count_y - 1, count_y)

    loads = []
    for half in range(2):
        cols = pl.ds(half * LANES, LANES)
        sources = [h_in.at[:, :, cols], vel_in.at[0, :, :, cols], vel_in.at[1, :, :, cols]]
        for item in range(3):
            loads.append(pltpu.make_async_copy(sources[item], own.at[item, half], load_sem.at[half, item]))
        for item, source in enumerate((bottom_in, coriolis_in)):
            loads.append(
                pltpu.make_async_copy(
                    source.at[:, cols], fixed.at[item, half, pl.ds(SUB, rows)], load_sem.at[half, 3 + item]
                )
            )
    loads.append(pltpu.make_async_copy(reduced_in, reduced_local, small_sem))
    row_loads = []
    for item in range(3):
        for lev in range(levels):
            source = h_in.at[lev] if item == 0 else vel_in.at[item - 1, lev]
            row_loads.append(
                pltpu.make_async_copy(source, by_row.at[item, pl.ds(2, rows), lev], row_sem.at[item, lev])
            )
    for copy in loads + row_loads:
        copy.start()

    barrier = pltpu.get_barrier_semaphore()

    def greet(x, y):
        pl.semaphore_signal(barrier, inc=1, device_id={"gx": x, "gy": y}, device_id_type=MESH)

    greet(me_x, north)
    greet(me_x, south)

    @pl.when(west_open)
    def _():
        for y in (north, me_y, south):
            greet(me_x - 1, y)

    @pl.when(east_open)
    def _():
        for y in (north, me_y, south):
            greet(me_x + 1, y)

    @pl.when(jnp.logical_not(west_open))
    def _():
        west_pack[...] = jnp.zeros_like(west_pack)

    @pl.when(jnp.logical_not(east_open))
    def _():
        east_pack[...] = jnp.zeros_like(east_pack)

    lane = lax.broadcasted_iota(jnp.int32, (SUB, LANES), 1)
    sub = lax.broadcasted_iota(jnp.int32, (SUB, LANES), 0)
    level = levels - 1 - lane // GROUP
    place = lane % GROUP
    for copy in loads:
        copy.wait()
    reduced_main = jnp.zeros((SUB, LANES), jnp.float32)
    reduced_strip = jnp.zeros((SUB, LANES), jnp.float32)
    for item in range(levels):
        value = 2.0 * reduced_local[item]
        reduced_main = jnp.where(sub == item, value, reduced_main)
        reduced_strip = jnp.where(level == item, value, reduced_strip)

    def turn(values, shift):
        return pltpu.roll(values, shift % LANES, 1)

    wall_last = jnp.logical_and(place == 13, jnp.logical_not(east_open))

    def spread(gathered):
        left = turn(gathered, -6)
        right = turn(gathered, 6)
        return jnp.where(place < 8, left, right)

    def build(block, _):
        base = pl.multiple_of(block * SUB, SUB)
        after = pl.multiple_of(block * SUB + SUB, SUB)
        made = []
        for item in range(3):
            gathered = jnp.zeros((SUB, LANES), jnp.float32)
            for lev in range(levels):
                low = own[item, 0, lev, pl.ds(base, SUB), :]
                high = own[item, 1, lev, pl.ds(base, SUB), :]
                joined = jnp.where(lane < LANES // 2, low, high)
                gathered = jnp.where(level == lev, turn(joined, GROUP * (levels - 1 - lev) + 8), gathered)
            value = spread(gathered)
            if item == 1:
                value = jnp.where(wall_last, 0.0, value)
            made.append(value)
        for item in range(2):
            low = fixed[item, 0, pl.ds(after, SUB), :]
            high = fixed[item, 1, pl.ds(after, SUB), :]
            joined = turn(jnp.where(lane < LANES // 2, low, high), 8)
            gathered = jnp.where(lane < GROUP, joined, 0.0)
            for shift in (16, 32, 64):
                gathered = gathered + turn(gathered, shift)
            made.append(spread(gathered))
        for item in range(5):
            strip[item, pl.ds(after, SUB), :] = made[item]
        eastbound = turn(made[4], -4)
        westbound = turn(made[4], 4)
        for item in (3, 2, 1, 0):
            eastbound = jnp.where(place < 2 * item + 2, turn(made[item], 2 * item - 12), eastbound)
            westbound = jnp.where(place >= 14 - 2 * item, turn(made[item], 12 - 2 * item), westbound)
        pack[0, pl.ds(base, SUB), :] = eastbound
        pack[1, pl.ds(base, SUB), :] = westbound
        return 0

    lax.fori_loop(0, blocks, build, 0, unroll=4)
    for copy in row_loads:
        copy.wait()

    first = pl.ds(0, SUB)
    last = pl.ds(rows - SUB, SUB)
    own_first = pl.ds(SUB, SUB)
    own_last = pl.ds(rows, SUB)
    ext_last = pl.ds(rows + SUB, SUB)
    ext_own = pl.ds(SUB, rows)

    def remote(index, source, target, x, y):
        return pltpu.make_async_remote_copy(
            src_ref=source,
            dst_ref=target,
            send_sem=send_sem.at[index],
            recv_sem=recv_sem.at[index],
            device_id={"gx": x, "gy": y},
            device_id_type=MESH,
        )

    along_y = [
        remote(0, by_row.at[:, pl.ds(rows, 2)], by_row.at[:, pl.ds(0, 2)], me_x, north),
        remote(1, by_row.at[:, pl.ds(2, 2)], by_row.at[:, pl.ds(rows + 2, 2)], me_x, south),
        remote(2, fixed.at[:, :, own_last], fixed.at[:, :, first], me_x, north),
        remote(3, fixed.at[:, :, own_first], fixed.at[:, :, ext_last], me_x, south),
        remote(4, strip.at[:, own_last], strip.at[:, first], me_x, north),
        remote(5, strip.at[:, own_first], strip.at[:, ext_last], me_x, south),
    ]
    to_east = [
        remote(6, pack.at[0], west_pack.at[ext_own], me_x + 1, me_y),
        remote(7, pack.at[0, last], west_pack.at[first], me_x + 1, north),
        remote(8, pack.at[0, first], west_pack.at[ext_last], me_x + 1, south),
    ]
    to_west = [
        remote(9, pack.at[1], east_pack.at[ext_own], me_x - 1, me_y),
        remote(10, pack.at[1, last], east_pack.at[first], me_x - 1, north),
        remote(11, pack.at[1, first], east_pack.at[ext_last], me_x - 1, south),
    ]

    greeted = 2 + 3 * west_open.astype(jnp.int32) + 3 * east_open.astype(jnp.int32)
    pl.semaphore_wait(barrier, greeted)
    for copy in along_y:
        copy.start()

    @pl.when(east_open)
    def _():
        for copy in to_east:
            copy.start()

    @pl.when(west_open)
    def _():
        for copy in to_west:
            copy.start()

    before_end = lane < LANES - 1
    at_start = lane == 0

    def eastward(pair):
        low, high = turn(pair[0], -1), turn(pair[1], -1)
        return [jnp.where(before_end, low, high), high]

    def westward(pair):
        low, high = turn(pair[0], 1), turn(pair[1], 1)
        return [low, jnp.where(at_start, low, high)]

    def each(function, *pairs):
        return [function(*items) for items in zip(*pairs)]

    def begin(row):
        thick, along_x, along_y = row
        wide = each(lambda a, b: a + b, thick, eastward(thick))
        flux = each(lambda a, b: a * b, wide, along_x)
        zero = [jnp.zeros((SUB, LANES), jnp.float32)] * 2
        return [thick, along_x, along_y, wide, flux, zero, zero, zero]

    def advance(carry, following, bottom_next, coriolis):
        thick, along_x, along_y, wide, flux, bern, flux_y_before, turn_before = carry
        thick_n, along_x_n, along_y_n = following
        wide_n = each(lambda a, b: a + b, thick_n, eastward(thick_n))
        flux_n = each(lambda a, b: a * b, wide_n, along_x_n)
        flux_y = each(lambda a, b, c: (a + b) * c, thick, thick_n, along_y)
        vort = each(
            lambda e, v, un, u, f: (e - v) - (un - u) + f,
            eastward(along_y), along_y, along_x_n, along_x, coriolis,
        )
        spin = each(lambda z, a, b: z / (a + b), vort, wide, wide_n)
        turn_y = each(lambda w, a, b: w * (a + b), spin, flux_y, eastward(flux_y))
        turn_x = each(lambda w, a, b: w * (a + b), spin, flux, flux_n)
        square = each(lambda a: a * a, along_x_n)
        bern_n = each(
            lambda s, w, vn, v, b, h: 0.5 * ((s + w) + (vn * vn + v * v))
            + (b + jnp.sum(h, axis=0, keepdims=True))
            + reduced_main * h,
            square, westward(square), along_y_n, along_y, bottom_next, thick_n,
        )
        rate_h = each(
            lambda f, w, g, p: -((f - w) + (g - p)), flux, westward(flux), flux_y, flux_y_before
        )
        rate_u = each(lambda p, t, e, b: (p + t) - (e - b), turn_before, turn_y, eastward(bern), bern)
        rate_v = each(lambda w, t, n, b: -(w + t) - (n - b), westward(turn_x), turn_x, bern_n, bern)
        carry = [thick_n, along_x_n, along_y_n, wide_n, flux_n, bern_n, flux_y, turn_y]
        return carry, [rate_h, rate_u, rate_v]

    def fixed_row(item, row):
        return [
            jnp.broadcast_to(fixed[item, half, pl.ds(row + SUB, 1), :], (SUB, LANES)) for half in range(2)
        ]

    def halves(ref, item, row):
        return [ref[item, row, :, pl.ds(half * LANES, LANES)] for half in range(2)]

    def start_row(row):
        return [halves(by_row, item, row + 2) for item in range(3)]

    def mid_row(row):
        return [halves(mid, item, row + 1) for item in range(3)]

    def keep_mid(row, carry, rates):
        for item in range(3):
            for half in range(2):
                value = carry[item][half] + 0.5 * time_step * rates[item][half]
                mid[item, row + 1, :, pl.ds(half * LANES, LANES)] = value

    def first_step(carry, row):
        after, rates = advance(carry, start_row(row + 1), fixed_row(0, row + 1), fixed_row(1, row))
        keep_mid(row, carry, rates)
        return after

    def sweep(carry, start, stop, step):
        whole = (stop - start) // UNROLL

        def some(block, carry):
            for extra in range(UNROLL):
                carry = step(carry, start + block * UNROLL + extra)
            return carry

        if whole:
            carry = lax.fori_loop(0, whole, some, carry)
        for row in range(start + whole * UNROLL, stop):
            carry = step(carry, row)
        return carry

    def first_sweep(start, stop):
        carry = begin(start_row(start - 1))
        carry, _ = advance(carry, start_row(start), fixed_row(0, start), fixed_row(1, start - 1))
        sweep(carry, start, stop, first_step)

    first_sweep(1, rows - 1)

    def second_step(carry, row):
        after, rates = advance(carry, mid_row(row + 1), fixed_row(0, row + 1), fixed_row(1, row))
        start = start_row(row)
        for item in range(3):
            for half in range(2):
                value = 0.5 * (start[item][half] + carry[item][half]) + 0.25 * time_step * rates[item][half]
                result[item, row, :, pl.ds(half * LANES, LANES)] = value
        return after

    def second_sweep(start, stop):
        carry = begin(mid_row(start - 1))
        carry, _ = advance(carry, mid_row(start), fixed_row(0, start), fixed_row(1, start - 1))
        sweep(carry, start, stop, second_step)

    second_sweep(2, rows - 2)

    for copy in along_y:
        copy.wait_recv()

    @pl.when(west_open)
    def _():
        for copy in to_east:
            copy.wait_recv()

    @pl.when(east_open)
    def _():
        for copy in to_west:
            copy.wait_recv()

    first_sweep(-1, 1)
    first_sweep(rows - 1, rows + 1)
    second_sweep(0, 2)
    second_sweep(rows - 2, rows)

    wide_lane = lax.broadcasted_iota(jnp.int32, (ext, LANES), 1)
    wide_place = wide_lane - (wide_lane // GROUP) * GROUP
    from_west = wide_place < 2
    from_east = wide_place >= 14
    outside = jnp.logical_or(
        jnp.logical_and(from_west, jnp.logical_not(west_open)),
        jnp.logical_and(from_east, jnp.logical_not(east_open)),
    )
    closed = jnp.logical_or(outside, jnp.logical_and(wide_place == 13, jnp.logical_not(east_open)))
    received_west = west_pack[...]
    received_east = east_pack[...]
    fields = []
    for item in range(5):
        value = jnp.where(from_west, turn(received_west, -2 * item), strip[item])
        fields.append(jnp.where(from_east, turn(received_east, 2 * item), value))
    weight = jnp.concatenate([reduced_strip] * (ext // SUB), axis=0)

    def strip_rates(thick, along_x, along_y, bottom, coriolis):
        def north_of(values):
            return pltpu.roll(values, ext - 1, 0)

        def south_of(values):
            return pltpu.roll(values, 1, 0)

        wide = thick + turn(thick, -1)
        flux = wide * along_x
        flux_y = (thick + north_of(thick)) * along_y
        vort = (turn(along_y, -1) - along_y) - (north_of(along_x) - along_x) + coriolis
        spin = vort / (wide + north_of(wide))
        turn_y = spin * (flux_y + turn(flux_y, -1))
        turn_x = spin * (flux + north_of(flux))
        square = along_x * along_x
        square_y = along_y * along_y
        total = thick
        for shift in (16, 32, 64):
            total = total + turn(total, shift)
        bern = 0.5 * ((square + turn(square, 1)) + (square_y + south_of(square_y))) + (bottom + total) + weight * thick
        rate_h = -((flux - turn(flux, 1)) + (flux_y - south_of(flux_y)))
        rate_u = (south_of(turn_y) + turn_y) - (turn(bern, -1) - bern)
        rate_v = -(turn(turn_x, 1) + turn_x) - (north_of(bern) - bern)
        return rate_h, rate_u, rate_v

    rates = strip_rates(*fields)
    middle = []
    for item in range(3):
        value = fields[item] + 0.5 * time_step * rates[item]
        middle.append(jnp.where(closed if item == 1 else outside, 0.0, value))
    rates = strip_rates(*middle, fields[3], fields[4])
    for item in range(3):
        value = 0.5 * (fields[item] + middle[item]) + 0.25 * time_step * rates[item]
        if item == 1:
            value = jnp.where(closed, 0.0, value)
        strip_out[item] = jnp.where(wide_place < 8, turn(value, -6), turn(value, 6))

    for copy in along_y:
        copy.wait_send()

    @pl.when(east_open)
    def _():
        for copy in to_east:
            copy.wait_send()

    @pl.when(west_open)
    def _():
        for copy in to_west:
            copy.wait_send()


def finish(rows, result, strip_out, h_out, vel_out, merged, store_sem):
    levels = SUB
    lane = lax.broadcasted_iota(jnp.int32, (SUB, LANES), 1)
    size = rows // GROUPS

    stores = []
    for group in range(GROUPS):

        def merge(step, _):
            row = group * size + step
            for item in range(3):
                value = jnp.broadcast_to(strip_out[item, pl.ds(row + SUB, 1), :], (SUB, LANES))
                moved = pltpu.roll(value, SUB, 1, stride=GROUP, stride_axis=0)
                low = result[item, row, :, pl.ds(0, LANES)]
                high = result[item, row, :, pl.ds(LANES, LANES)]
                merged[item, row, :, pl.ds(0, LANES)] = jnp.where(lane < 2, moved, low)
                merged[item, row, :, pl.ds(LANES, LANES)] = jnp.where(lane >= LANES - 4, moved, high)
            return 0

        lax.fori_loop(0, size, merge, 0, unroll=SUB)
        part = pl.ds(group * size, size)
        for item in range(3):
            for lev in range(levels):
                target = h_out.at[lev, part] if item == 0 else vel_out.at[item - 1, lev, part]
                copy = pltpu.make_async_copy(
                    merged.at[item, part, lev], target, store_sem.at[group, item, lev]
                )
                copy.start()
                stores.append(copy)
    for copy in stores:
        copy.wait()


def solution(mesh):
    count_x, count_y = mesh.shape["gx"], mesh.shape["gy"]

    def body(thickness, velocity, bottom, coriolis, reduced):
        levels, rows, columns = thickness.shape
        assert levels == SUB and columns == 2 * LANES and rows % SUB == 0
        ext = rows + 2 * SUB
        f32 = jnp.float32

        def run(*refs):
            kernel(count_x, count_y, rows, *refs)

        in_hbm = pl.BlockSpec(memory_space=pltpu.HBM)
        in_vmem = pl.BlockSpec(memory_space=pltpu.VMEM)
        result, strip_out = pl.pallas_call(
            run,
            out_shape=(
                pltpu.VMEM((3, rows, levels, columns), f32),
                pltpu.VMEM((3, ext, LANES), f32),
            ),
            in_specs=[in_hbm] * 5,
            out_specs=(in_vmem, in_vmem),
            scratch_shapes=[
                pltpu.VMEM((3, 2, levels, rows, LANES), f32),
                pltpu.VMEM((3, rows + 4, levels, columns), f32),
                pltpu.VMEM((3, rows + 2, levels, columns), f32),
                pltpu.VMEM((2, 2, ext, LANES), f32),
                pltpu.VMEM((5, ext, LANES), f32),
                pltpu.VMEM((2, rows, LANES), f32),
                pltpu.VMEM((ext, LANES), f32),
                pltpu.VMEM((ext, LANES), f32),
                pltpu.SMEM((levels,), f32),
                pltpu.SemaphoreType.DMA((2, 5)),
                pltpu.SemaphoreType.DMA,
                pltpu.SemaphoreType.DMA((3, levels)),
                pltpu.SemaphoreType.DMA((12,)),
                pltpu.SemaphoreType.DMA((12,)),
            ],
            compiler_params=pltpu.CompilerParams(
                collective_id=0, has_side_effects=True, vmem_limit_bytes=VMEM_MAIN
            ),
            cost_estimate=pl.CostEstimate(
                flops=200 * thickness.size, bytes_accessed=28 * thickness.size, transcendentals=0
            ),
        )(thickness, velocity, bottom, coriolis, reduced)

        def end(*refs):
            finish(rows, *refs)

        return pl.pallas_call(
            end,
            out_shape=(
                jax.ShapeDtypeStruct(thickness.shape, f32),
                jax.ShapeDtypeStruct(velocity.shape, f32),
            ),
            in_specs=[in_vmem] * 2,
            out_specs=(in_hbm, in_hbm),
            scratch_shapes=[
                pltpu.VMEM((3, rows, levels, columns), f32),
                pltpu.SemaphoreType.DMA((GROUPS, 3, levels)),
            ],
            compiler_params=pltpu.CompilerParams(vmem_limit_bytes=VMEM_END),
            cost_estimate=pl.CostEstimate(
                flops=thickness.size, bytes_accessed=24 * thickness.size, transcendentals=0
            ),
        )(result, strip_out)

    return jax.shard_map(
        body,
        mesh=mesh,
        in_specs=(P(None, "gy", "gx"), P(None, None, "gy", "gx"), P("gy", "gx"), P("gy", "gx"), P()),
        out_specs=(P(None, "gy", "gx"), P(None, None, "gy", "gx")),
        check_vma=False,
    )
```

```python
import jax
import jax.numpy as jnp
from jax import lax
from jax.experimental import pallas as pl
from jax.experimental.pallas import tpu as pltpu
from jax.sharding import PartitionSpec as P

time_step = 0.1
LANES = 128
SUB = 8
GROUP = 16
UNROLL = 10
VMEM_MAIN = 58 * 1024 * 1024
VMEM_END = 16 * 1024 * 1024
MESH = pl.DeviceIdType.MESH


def kernel(
    count_x, count_y, rows,
    h_in, vel_in, bottom_in, coriolis_in, reduced_in,
    result, strip_out,
    own, by_row, mid, halo, fixed, strip, pack, west_pack, east_pack,
    reduced_local, load_sem, fixed_sem, small_sem, row_sem, send_sem, recv_sem,
):
    levels = SUB
    blocks = rows // SUB
    ext = rows + 2 * SUB
    me_x = lax.axis_index("gx")
    me_y = lax.axis_index("gy")
    west_open = me_x > 0
    east_open = me_x < count_x - 1
    north = lax.rem(me_y + 1, count_y)
    south = lax.rem(me_y + count_y - 1, count_y)

    loads = []
    for half in range(2):
        cols = pl.ds(half * LANES, LANES)
        sources = [h_in.at[:, :, cols], vel_in.at[0, :, :, cols], vel_in.at[1, :, :, cols]]
        for item in range(3):
            loads.append(pltpu.make_async_copy(sources[item], own.at[item, half], load_sem.at[half, item]))
    for item, source in enumerate((bottom_in, coriolis_in)):
        for half in range(2):
            cols = pl.ds(half * LANES, LANES)
            target = fixed.at[item, half, pl.ds(SUB, rows)]
            loads.append(pltpu.make_async_copy(source.at[:, cols], target, fixed_sem.at[item, half]))
    loads.append(pltpu.make_async_copy(reduced_in, reduced_local, small_sem))
    row_loads = []
    for item in range(3):
        for lev in range(levels):
            source = h_in.at[lev] if item == 0 else vel_in.at[item - 1, lev]
            row_loads.append(
                pltpu.make_async_copy(source, by_row.at[item, :, lev], row_sem.at[item, lev])
            )
    for copy in loads + row_loads:
        copy.start()

    barrier = pltpu.get_barrier_semaphore()

    def greet(x, y):
        pl.semaphore_signal(barrier, inc=1, device_id={"gx": x, "gy": y}, device_id_type=MESH)

    greet(me_x, north)
    greet(me_x, south)

    @pl.when(west_open)
    def _():
        for y in (north, me_y, south):
            greet(me_x - 1, y)

    @pl.when(east_open)
    def _():
        for y in (north, me_y, south):
            greet(me_x + 1, y)

    @pl.when(jnp.logical_not(west_open))
    def _():
        west_pack[...] = jnp.zeros_like(west_pack)

    @pl.when(jnp.logical_not(east_open))
    def _():
        east_pack[...] = jnp.zeros_like(east_pack)

    lane = lax.broadcasted_iota(jnp.int32, (SUB, LANES), 1)
    sub = lax.broadcasted_iota(jnp.int32, (SUB, LANES), 0)
    level = levels - 1 - lane // GROUP
    place = lane % GROUP
    for copy in loads:
        copy.wait()
    reduced_main = jnp.zeros((SUB, LANES), jnp.float32)
    reduced_strip = jnp.zeros((SUB, LANES), jnp.float32)
    for item in range(levels):
        value = 2.0 * reduced_local[item]
        reduced_main = jnp.where(sub == item, value, reduced_main)
        reduced_strip = jnp.where(level == item, value, reduced_strip)

    def turn(values, shift):
        return pltpu.roll(values, shift % LANES, 1)

    wall_last = jnp.logical_and(place == 13, jnp.logical_not(east_open))

    def spread(gathered):
        left = turn(gathered, -6)
        right = turn(gathered, 6)
        return jnp.where(place < 8, left, right)

    def build(read, after):
        made = []
        for item in range(3):
            gathered = jnp.zeros((SUB, LANES), jnp.float32)
            for lev in range(levels):
                joined = jnp.where(lane < LANES // 2, read(item, 0, lev), read(item, 1, lev))
                moved = turn(joined, GROUP * (levels - 1 - lev) + 8)
                gathered = jnp.where(level == lev, moved, gathered)
            value = spread(gathered)
            if item == 1:
                value = jnp.where(wall_last, 0.0, value)
            made.append(value)
        for item in range(2):
            low = fixed[item, 0, pl.ds(after, SUB), :]
            high = fixed[item, 1, pl.ds(after, SUB), :]
            joined = turn(jnp.where(lane < LANES // 2, low, high), 8)
            gathered = jnp.where(lane < GROUP, joined, 0.0)
            for shift in (16, 32, 64):
                gathered = gathered + turn(gathered, shift)
            made.append(spread(gathered))
        for item in range(5):
            strip[item, pl.ds(after, SUB), :] = made[item]
        return made

    def build_own(block, _):
        base = pl.multiple_of(block * SUB, SUB)
        after = pl.multiple_of(block * SUB + SUB, SUB)
        made = build(lambda item, half, lev: own[item, half, lev, pl.ds(base, SUB), :], after)
        eastbound = turn(made[4], -4)
        westbound = turn(made[4], 4)
        for item in (3, 2, 1, 0):
            eastbound = jnp.where(place < 2 * item + 2, turn(made[item], 2 * item - 12), eastbound)
            westbound = jnp.where(place >= 14 - 2 * item, turn(made[item], 12 - 2 * item), westbound)
        pack[0, pl.ds(base, SUB), :] = eastbound
        pack[1, pl.ds(base, SUB), :] = westbound
        return 0

    lax.fori_loop(0, blocks, build_own, 0, unroll=4)
    for copy in row_loads:
        copy.wait()

    first = pl.ds(0, SUB)
    last = pl.ds(rows - SUB, SUB)
    ext_last = pl.ds(rows + SUB, SUB)
    ext_own = pl.ds(SUB, rows)

    def remote(index, source, target, x, y):
        return pltpu.make_async_remote_copy(
            src_ref=source,
            dst_ref=target,
            send_sem=send_sem.at[index],
            recv_sem=recv_sem.at[index],
            device_id={"gx": x, "gy": y},
            device_id_type=MESH,
        )

    along_y = []
    for side, (source_row, row, y) in enumerate(((rows - 2, SUB - 2, north), (0, 0, south))):
        pair, place_there = pl.ds(source_row, 2), pl.ds(row, 2)
        copies = []
        for half in range(2):
            cols = pl.ds(half * LANES, LANES)
            copies.append((h_in.at[:, pair, cols], halo.at[side, 0, half, :, place_there]))
            copies.append((vel_in.at[:, :, pair, cols], halo.at[side, pl.ds(1, 2), half, :, place_there]))
            outer = pl.ds(row + side * (rows + SUB), 2)
            copies.append((bottom_in.at[pair, cols], fixed.at[0, half, outer]))
            copies.append((coriolis_in.at[pair, cols], fixed.at[1, half, outer]))
        for source, target in copies:
            along_y.append(remote(6 + len(along_y), source, target, me_x, y))
    to_east = [
        remote(0, pack.at[0], west_pack.at[ext_own], me_x + 1, me_y),
        remote(1, pack.at[0, last], west_pack.at[first], me_x + 1, north),
        remote(2, pack.at[0, first], west_pack.at[ext_last], me_x + 1, south),
    ]
    to_west = [
        remote(3, pack.at[1], east_pack.at[ext_own], me_x - 1, me_y),
        remote(4, pack.at[1, last], east_pack.at[first], me_x - 1, north),
        remote(5, pack.at[1, first], east_pack.at[ext_last], me_x - 1, south),
    ]

    before_end = lane < LANES - 1
    at_start = lane == 0

    def eastward(pair):
        low, high = turn(pair[0], -1), turn(pair[1], -1)
        return [jnp.where(before_end, low, high), high]

    def westward(pair):
        low, high = turn(pair[0], 1), turn(pair[1], 1)
        return [low, jnp.where(at_start, low, high)]

    def each(function, *pairs):
        return [function(*items) for items in zip(*pairs)]

    def begin(row):
        thick, along_x, along_y = row
        wide = each(lambda a, b: a + b, thick, eastward(thick))
        flux = each(lambda a, b: a * b, wide, along_x)
        zero = [jnp.zeros((SUB, LANES), jnp.float32)] * 2
        return [thick, along_x, along_y, wide, flux, zero, zero, zero]

    def advance(carry, following, bottom_next, coriolis):
        thick, along_x, along_y, wide, flux, bern, flux_y_before, turn_before = carry
        thick_n, along_x_n, along_y_n = following
        wide_n = each(lambda a, b: a + b, thick_n, eastward(thick_n))
        flux_n = each(lambda a, b: a * b, wide_n, along_x_n)
        flux_y = each(lambda a, b, c: (a + b) * c, thick, thick_n, along_y)
        vort = each(
            lambda e, v, un, u, f: (e - v) - (un - u) + f,
            eastward(along_y), along_y, along_x_n, along_x, coriolis,
        )
        spin = each(lambda z, a, b: z / (a + b), vort, wide, wide_n)
        turn_y = each(lambda w, a, b: w * (a + b), spin, flux_y, eastward(flux_y))
        turn_x = each(lambda w, a, b: w * (a + b), spin, flux, flux_n)
        square = each(lambda a: a * a, along_x_n)
        bern_n = each(
            lambda s, w, vn, v, b, h: 0.5 * ((s + w) + (vn * vn + v * v))
            + (b + jnp.sum(h, axis=0, keepdims=True))
            + reduced_main * h,
            square, westward(square), along_y_n, along_y, bottom_next, thick_n,
        )
        rate_h = each(
            lambda f, w, g, p: -((f - w) + (g - p)), flux, westward(flux), flux_y, flux_y_before
        )
        rate_u = each(lambda p, t, e, b: (p + t) - (e - b), turn_before, turn_y, eastward(bern), bern)
        rate_v = each(lambda w, t, n, b: -(w + t) - (n - b), westward(turn_x), turn_x, bern_n, bern)
        carry = [thick_n, along_x_n, along_y_n, wide_n, flux_n, bern_n, flux_y, turn_y]
        return carry, [rate_h, rate_u, rate_v]

    def fixed_row(item, row):
        return [
            jnp.broadcast_to(fixed[item, half, pl.ds(row + SUB, 1), :], (SUB, LANES)) for half in range(2)
        ]

    def halves(ref, item, row):
        return [ref[item, row, :, pl.ds(half * LANES, LANES)] for half in range(2)]

    def start_row(row):
        if isinstance(row, int) and not 0 <= row < rows:
            side, line = (0, row + SUB) if row < 0 else (1, row - rows)
            return [
                [
                    halo.at[side, item, half].reshape(levels * SUB, LANES)[pl.ds(line, levels, stride=SUB), :]
                    for half in range(2)
                ]
                for item in range(3)
            ]
        return [halves(by_row, item, row) for item in range(3)]

    def mid_row(row):
        return [halves(mid, item, row + 1) for item in range(3)]

    def keep_mid(row, carry, rates):
        for item in range(3):
            for half in range(2):
                value = carry[item][half] + 0.5 * time_step * rates[item][half]
                mid[item, row + 1, :, pl.ds(half * LANES, LANES)] = value

    def first_step(carry, row):
        after, rates = advance(carry, start_row(row + 1), fixed_row(0, row + 1), fixed_row(1, row))
        keep_mid(row, carry, rates)
        return after

    def sweep(carry, start, stop, step):
        whole = (stop - start) // UNROLL

        def some(block, carry):
            for extra in range(UNROLL):
                carry = step(carry, start + block * UNROLL + extra)
            return carry

        if whole:
            carry = lax.fori_loop(0, whole, some, carry)
        for row in range(start + whole * UNROLL, stop):
            carry = step(carry, row)
        return carry

    def first_begin(start):
        carry = begin(start_row(start - 1))
        carry, _ = advance(carry, start_row(start), fixed_row(0, start), fixed_row(1, start - 1))
        return carry

    carry = first_begin(1)
    early = 1 + UNROLL * ((rows - 2) // (2 * UNROLL))
    carry = sweep(carry, 1, early, first_step)

    greeted = 2 + 3 * west_open.astype(jnp.int32) + 3 * east_open.astype(jnp.int32)
    pl.semaphore_wait(barrier, greeted)
    for copy in along_y:
        copy.start()

    @pl.when(east_open)
    def _():
        for copy in to_east:
            copy.start()

    @pl.when(west_open)
    def _():
        for copy in to_west:
            copy.start()

    sweep(carry, early, rows - 1, first_step)

    out_flat = [[result.at[item, half].reshape(levels * rows, LANES) for half in range(2)] for item in range(3)]

    def second_step(carry, row):
        after, rates = advance(carry, mid_row(row + 1), fixed_row(0, row + 1), fixed_row(1, row))
        start = start_row(row)
        for item in range(3):
            for half in range(2):
                value = 0.5 * (start[item][half] + carry[item][half]) + 0.25 * time_step * rates[item][half]
                out_flat[item][half][pl.ds(row, levels, stride=rows), :] = value
        return after

    def second_sweep(start, stop):
        carry = begin(mid_row(start - 1))
        carry, _ = advance(carry, mid_row(start), fixed_row(0, start), fixed_row(1, start - 1))
        sweep(carry, start, stop, second_step)

    second_sweep(2, rows - 2)

    for copy in along_y:
        copy.wait_recv()

    @pl.when(west_open)
    def _():
        for copy in to_east:
            copy.wait_recv()

    @pl.when(east_open)
    def _():
        for copy in to_west:
            copy.wait_recv()

    sweep(first_begin(-1), -1, 1, first_step)
    sweep(first_begin(rows - 1), rows - 1, rows + 1, first_step)
    second_sweep(0, 2)
    second_sweep(rows - 2, rows)
    for side, after in ((0, 0), (1, rows + SUB)):
        build(lambda item, half, lev: halo[side, item, half, lev], after)

    wide_lane = lax.broadcasted_iota(jnp.int32, (ext, LANES), 1)
    wide_place = wide_lane - (wide_lane // GROUP) * GROUP
    from_west = wide_place < 2
    from_east = wide_place >= 14
    outside = jnp.logical_or(
        jnp.logical_and(from_west, jnp.logical_not(west_open)),
        jnp.logical_and(from_east, jnp.logical_not(east_open)),
    )
    closed = jnp.logical_or(outside, jnp.logical_and(wide_place == 13, jnp.logical_not(east_open)))
    received_west = west_pack[...]
    received_east = east_pack[...]
    fields = []
    for item in range(5):
        value = jnp.where(from_west, turn(received_west, -2 * item), strip[item])
        fields.append(jnp.where(from_east, turn(received_east, 2 * item), value))
    weight = jnp.concatenate([reduced_strip] * (ext // SUB), axis=0)

    def strip_rates(thick, along_x, along_y, bottom, coriolis):
        def north_of(values):
            return pltpu.roll(values, ext - 1, 0)

        def south_of(values):
            return pltpu.roll(values, 1, 0)

        wide = thick + turn(thick, -1)
        flux = wide * along_x
        flux_y = (thick + north_of(thick)) * along_y
        vort = (turn(along_y, -1) - along_y) - (north_of(along_x) - along_x) + coriolis
        spin = vort / (wide + north_of(wide))
        turn_y = spin * (flux_y + turn(flux_y, -1))
        turn_x = spin * (flux + north_of(flux))
        square = along_x * along_x
        square_y = along_y * along_y
        total = thick
        for shift in (16, 32, 64):
            total = total + turn(total, shift)
        bern = 0.5 * ((square + turn(square, 1)) + (square_y + south_of(square_y))) + (bottom + total) + weight * thick
        rate_h = -((flux - turn(flux, 1)) + (flux_y - south_of(flux_y)))
        rate_u = (south_of(turn_y) + turn_y) - (turn(bern, -1) - bern)
        rate_v = -(turn(turn_x, 1) + turn_x) - (north_of(bern) - bern)
        return rate_h, rate_u, rate_v

    rates = strip_rates(*fields)
    middle = []
    for item in range(3):
        value = fields[item] + 0.5 * time_step * rates[item]
        middle.append(jnp.where(closed if item == 1 else outside, 0.0, value))
    rates = strip_rates(*middle, fields[3], fields[4])
    for item in range(3):
        value = 0.5 * (fields[item] + middle[item]) + 0.25 * time_step * rates[item]
        if item == 1:
            value = jnp.where(closed, 0.0, value)
        strip_out[item] = jnp.where(wide_place < 8, turn(value, -6), turn(value, 6))

    for copy in along_y:
        copy.wait_send()

    @pl.when(east_open)
    def _():
        for copy in to_east:
            copy.wait_send()

    @pl.when(west_open)
    def _():
        for copy in to_west:
            copy.wait_send()


def finish(rows, result, strip_out, h_out, vel_out, merged, store_sem):
    levels = SUB
    blocks = rows // SUB
    lane = lax.broadcasted_iota(jnp.int32, (SUB, LANES), 1)

    stores = []
    for block in range(blocks):
        part = pl.ds(block * SUB, SUB)
        for item in range(3):
            value = strip_out[item, pl.ds(block * SUB + SUB, SUB), :]
            for lev in range(levels):
                moved = pltpu.roll(value, (SUB + GROUP * lev) % LANES, 1)
                low = result[item, 0, lev, part, :]
                high = result[item, 1, lev, part, :]
                merged[item, lev, part, pl.ds(0, LANES)] = jnp.where(lane < 2, moved, low)
                merged[item, lev, part, pl.ds(LANES, LANES)] = jnp.where(lane >= LANES - 4, moved, high)
        targets = [h_out.at[:, part], vel_out.at[0, :, part], vel_out.at[1, :, part]]
        for item in range(3):
            copy = pltpu.make_async_copy(merged.at[item, :, part], targets[item], store_sem.at[block, item])
            copy.start()
            stores.append(copy)
    for copy in stores:
        copy.wait()


def solution(mesh):
    count_x, count_y = mesh.shape["gx"], mesh.shape["gy"]

    def body(thickness, velocity, bottom, coriolis, reduced):
        levels, rows, columns = thickness.shape
        assert levels == SUB and columns == 2 * LANES and rows % SUB == 0
        ext = rows + 2 * SUB
        f32 = jnp.float32

        def run(*refs):
            kernel(count_x, count_y, rows, *refs)

        in_hbm = pl.BlockSpec(memory_space=pltpu.HBM)
        in_vmem = pl.BlockSpec(memory_space=pltpu.VMEM)
        result, strip_out = pl.pallas_call(
            run,
            out_shape=(
                pltpu.VMEM((3, 2, levels, rows, LANES), f32),
                pltpu.VMEM((3, ext, LANES), f32),
            ),
            in_specs=[in_hbm] * 5,
            out_specs=(in_vmem, in_vmem),
            scratch_shapes=[
                pltpu.VMEM((3, 2, levels, rows, LANES), f32),
                pltpu.VMEM((3, rows, levels, columns), f32),
                pltpu.VMEM((3, rows + 2, levels, columns), f32),
                pltpu.VMEM((2, 3, 2, levels, SUB, LANES), f32),
                pltpu.VMEM((2, 2, ext, LANES), f32),
                pltpu.VMEM((5, ext, LANES), f32),
                pltpu.VMEM((2, rows, LANES), f32),
                pltpu.VMEM((ext, LANES), f32),
                pltpu.VMEM((ext, LANES), f32),
                pltpu.SMEM((levels,), f32),
                pltpu.SemaphoreType.DMA((2, 3)),
                pltpu.SemaphoreType.DMA((2, 2)),
                pltpu.SemaphoreType.DMA,
                pltpu.SemaphoreType.DMA((3, levels)),
                pltpu.SemaphoreType.DMA((22,)),
                pltpu.SemaphoreType.DMA((22,)),
            ],
            compiler_params=pltpu.CompilerParams(
                collective_id=0, has_side_effects=True, vmem_limit_bytes=VMEM_MAIN
            ),
            cost_estimate=pl.CostEstimate(
                flops=200 * thickness.size, bytes_accessed=28 * thickness.size, transcendentals=0
            ),
        )(thickness, velocity, bottom, coriolis, reduced)

        def end(*refs):
            finish(rows, *refs)

        return pl.pallas_call(
            end,
            out_shape=(
                jax.ShapeDtypeStruct(thickness.shape, f32),
                jax.ShapeDtypeStruct(velocity.shape, f32),
            ),
            in_specs=[in_vmem] * 2,
            out_specs=(in_hbm, in_hbm),
            scratch_shapes=[
                pltpu.VMEM((3, levels, rows, columns), f32),
                pltpu.SemaphoreType.DMA((rows // SUB, 3)),
            ],
            compiler_params=pltpu.CompilerParams(vmem_limit_bytes=VMEM_END),
            cost_estimate=pl.CostEstimate(
                flops=thickness.size, bytes_accessed=24 * thickness.size, transcendentals=0
            ),
        )(result, strip_out)

    return jax.shard_map(
        body,
        mesh=mesh,
        in_specs=(P(None, "gy", "gx"), P(None, None, "gy", "gx"), P("gy", "gx"), P("gy", "gx"), P()),
        out_specs=(P(None, "gy", "gx"), P(None, None, "gy", "gx")),
        check_vma=False,
    )
```

```python
import jax
import jax.numpy as jnp
from jax import lax
from jax.experimental import pallas as pl
from jax.experimental.pallas import tpu as pltpu
from jax.sharding import PartitionSpec as P

time_step = 0.1
LANES = 128
SUB = 8
GROUP = 16
UNROLL = 10
VMEM_MAIN = 58 * 1024 * 1024
VMEM_END = 16 * 1024 * 1024
MESH = pl.DeviceIdType.MESH


def quotient(top, below):
    inverse = pl.reciprocal(below, approx=True)
    return top * (inverse * (2.0 - below * inverse))


def kernel(
    count_x, count_y, rows,
    h_in, vel_in, bottom_in, coriolis_in, reduced_in,
    result, strip_out,
    own, by_row, mid, halo, fixed, strip, pack, west_pack, east_pack,
    reduced_local, load_sem, fixed_sem, small_sem, row_sem, send_sem, recv_sem,
):
    levels = SUB
    blocks = rows // SUB
    ext = rows + 2 * SUB
    me_x = lax.axis_index("gx")
    me_y = lax.axis_index("gy")
    west_open = me_x > 0
    east_open = me_x < count_x - 1
    north = lax.rem(me_y + 1, count_y)
    south = lax.rem(me_y + count_y - 1, count_y)

    loads = []
    for half in range(2):
        cols = pl.ds(half * LANES, LANES)
        sources = [h_in.at[:, :, cols], vel_in.at[0, :, :, cols], vel_in.at[1, :, :, cols]]
        for item in range(3):
            loads.append(pltpu.make_async_copy(sources[item], own.at[item, half], load_sem.at[half, item]))
    for item, source in enumerate((bottom_in, coriolis_in)):
        for half in range(2):
            cols = pl.ds(half * LANES, LANES)
            target = fixed.at[item, half, pl.ds(SUB, rows)]
            loads.append(pltpu.make_async_copy(source.at[:, cols], target, fixed_sem.at[item, half]))
    loads.append(pltpu.make_async_copy(reduced_in, reduced_local, small_sem))
    row_loads = []
    for item in range(3):
        for lev in range(levels):
            source = h_in.at[lev] if item == 0 else vel_in.at[item - 1, lev]
            row_loads.append(
                pltpu.make_async_copy(source, by_row.at[item, :, lev], row_sem.at[item, lev])
            )
    for copy in loads + row_loads:
        copy.start()

    barrier = pltpu.get_barrier_semaphore()

    def greet(x, y):
        pl.semaphore_signal(barrier, inc=1, device_id={"gx": x, "gy": y}, device_id_type=MESH)

    greet(me_x, north)
    greet(me_x, south)

    @pl.when(west_open)
    def _():
        for y in (north, me_y, south):
            greet(me_x - 1, y)

    @pl.when(east_open)
    def _():
        for y in (north, me_y, south):
            greet(me_x + 1, y)

    @pl.when(jnp.logical_not(west_open))
    def _():
        west_pack[...] = jnp.zeros_like(west_pack)

    @pl.when(jnp.logical_not(east_open))
    def _():
        east_pack[...] = jnp.zeros_like(east_pack)

    lane = lax.broadcasted_iota(jnp.int32, (SUB, LANES), 1)
    sub = lax.broadcasted_iota(jnp.int32, (SUB, LANES), 0)
    level = levels - 1 - lane // GROUP
    place = lane % GROUP
    for copy in loads:
        copy.wait()
    reduced_main = jnp.zeros((SUB, LANES), jnp.float32)
    reduced_strip = jnp.zeros((SUB, LANES), jnp.float32)
    for item in range(levels):
        value = 2.0 * reduced_local[item]
        reduced_main = jnp.where(sub == item, value, reduced_main)
        reduced_strip = jnp.where(level == item, value, reduced_strip)

    def turn(values, shift):
        return pltpu.roll(values, shift % LANES, 1)

    wall_last = jnp.logical_and(place == 13, jnp.logical_not(east_open))

    def spread(gathered):
        left = turn(gathered, -6)
        right = turn(gathered, 6)
        return jnp.where(place < 8, left, right)

    def build(read, after):
        made = []
        for item in range(3):
            gathered = jnp.zeros((SUB, LANES), jnp.float32)
            for lev in range(levels):
                joined = jnp.where(lane < LANES // 2, read(item, 0, lev), read(item, 1, lev))
                moved = turn(joined, GROUP * (levels - 1 - lev) + 8)
                gathered = jnp.where(level == lev, moved, gathered)
            value = spread(gathered)
            if item == 1:
                value = jnp.where(wall_last, 0.0, value)
            made.append(value)
        for item in range(2):
            low = fixed[item, 0, pl.ds(after, SUB), :]
            high = fixed[item, 1, pl.ds(after, SUB), :]
            joined = turn(jnp.where(lane < LANES // 2, low, high), 8)
            gathered = jnp.where(lane < GROUP, joined, 0.0)
            for shift in (16, 32, 64):
                gathered = gathered + turn(gathered, shift)
            made.append(spread(gathered))
        for item in range(5):
            strip[item, pl.ds(after, SUB), :] = made[item]
        return made

    def build_own(block, _):
        base = pl.multiple_of(block * SUB, SUB)
        after = pl.multiple_of(block * SUB + SUB, SUB)
        made = build(lambda item, half, lev: own[item, half, lev, pl.ds(base, SUB), :], after)
        eastbound = turn(made[4], -4)
        westbound = turn(made[4], 4)
        for item in (3, 2, 1, 0):
            eastbound = jnp.where(place < 2 * item + 2, turn(made[item], 2 * item - 12), eastbound)
            westbound = jnp.where(place >= 14 - 2 * item, turn(made[item], 12 - 2 * item), westbound)
        pack[0, pl.ds(base, SUB), :] = eastbound
        pack[1, pl.ds(base, SUB), :] = westbound
        return 0

    lax.fori_loop(0, blocks, build_own, 0, unroll=4)
    for copy in row_loads:
        copy.wait()

    first = pl.ds(0, SUB)
    last = pl.ds(rows - SUB, SUB)
    ext_last = pl.ds(rows + SUB, SUB)
    ext_own = pl.ds(SUB, rows)

    def remote(index, source, target, x, y):
        return pltpu.make_async_remote_copy(
            src_ref=source,
            dst_ref=target,
            send_sem=send_sem.at[index],
            recv_sem=recv_sem.at[index],
            device_id={"gx": x, "gy": y},
            device_id_type=MESH,
        )

    along_y = []
    for side, (source_row, row, y) in enumerate(((rows - 2, SUB - 2, north), (0, 0, south))):
        pair, place_there = pl.ds(source_row, 2), pl.ds(row, 2)
        copies = []
        for half in range(2):
            cols = pl.ds(half * LANES, LANES)
            copies.append((h_in.at[:, pair, cols], halo.at[side, 0, half, :, place_there]))
            copies.append((vel_in.at[:, :, pair, cols], halo.at[side, pl.ds(1, 2), half, :, place_there]))
            outer = pl.ds(row + side * (rows + SUB), 2)
            copies.append((bottom_in.at[pair, cols], fixed.at[0, half, outer]))
            copies.append((coriolis_in.at[pair, cols], fixed.at[1, half, outer]))
        for source, target in copies:
            along_y.append(remote(6 + len(along_y), source, target, me_x, y))
    to_east = [
        remote(0, pack.at[0], west_pack.at[ext_own], me_x + 1, me_y),
        remote(1, pack.at[0, last], west_pack.at[first], me_x + 1, north),
        remote(2, pack.at[0, first], west_pack.at[ext_last], me_x + 1, south),
    ]
    to_west = [
        remote(3, pack.at[1], east_pack.at[ext_own], me_x - 1, me_y),
        remote(4, pack.at[1, last], east_pack.at[first], me_x - 1, north),
        remote(5, pack.at[1, first], east_pack.at[ext_last], me_x - 1, south),
    ]

    greeted = 2 + 3 * west_open.astype(jnp.int32) + 3 * east_open.astype(jnp.int32)
    pl.semaphore_wait(barrier, greeted)
    for copy in along_y:
        copy.start()

    @pl.when(east_open)
    def _():
        for copy in to_east:
            copy.start()

    @pl.when(west_open)
    def _():
        for copy in to_west:
            copy.start()

    before_end = lane < LANES - 1
    at_start = lane == 0

    def eastward(pair):
        low, high = turn(pair[0], -1), turn(pair[1], -1)
        return [jnp.where(before_end, low, high), high]

    def westward(pair):
        low, high = turn(pair[0], 1), turn(pair[1], 1)
        return [low, jnp.where(at_start, low, high)]

    def each(function, *pairs):
        return [function(*items) for items in zip(*pairs)]

    def begin(row):
        thick, along_x, along_y = row
        wide = each(lambda a, b: a + b, thick, eastward(thick))
        flux = each(lambda a, b: a * b, wide, along_x)
        zero = [jnp.zeros((SUB, LANES), jnp.float32)] * 2
        return [thick, along_x, along_y, wide, flux, zero, zero, zero]

    def advance(carry, following, bottom_next, coriolis):
        thick, along_x, along_y, wide, flux, bern, flux_y_before, turn_before = carry
        thick_n, along_x_n, along_y_n = following
        wide_n = each(lambda a, b: a + b, thick_n, eastward(thick_n))
        flux_n = each(lambda a, b: a * b, wide_n, along_x_n)
        flux_y = each(lambda a, b, c: (a + b) * c, thick, thick_n, along_y)
        vort = each(
            lambda e, v, un, u, f: (e - v) - (un - u) + f,
            eastward(along_y), along_y, along_x_n, along_x, coriolis,
        )
        spin = each(lambda z, a, b: quotient(z, a + b), vort, wide, wide_n)
        turn_y = each(lambda w, a, b: w * (a + b), spin, flux_y, eastward(flux_y))
        turn_x = each(lambda w, a, b: w * (a + b), spin, flux, flux_n)
        square = each(lambda a: a * a, along_x_n)
        bern_n = each(
            lambda s, w, vn, v, b, h: 0.5 * ((s + w) + (vn * vn + v * v))
            + (b + jnp.sum(h, axis=0, keepdims=True))
            + reduced_main * h,
            square, westward(square), along_y_n, along_y, bottom_next, thick_n,
        )
        rate_h = each(
            lambda f, w, g, p: -((f - w) + (g - p)), flux, westward(flux), flux_y, flux_y_before
        )
        rate_u = each(lambda p, t, e, b: (p + t) - (e - b), turn_before, turn_y, eastward(bern), bern)
        rate_v = each(lambda w, t, n, b: -(w + t) - (n - b), westward(turn_x), turn_x, bern_n, bern)
        carry = [thick_n, along_x_n, along_y_n, wide_n, flux_n, bern_n, flux_y, turn_y]
        return carry, [rate_h, rate_u, rate_v]

    def fixed_row(item, row):
        return [
            jnp.broadcast_to(fixed[item, half, pl.ds(row + SUB, 1), :], (SUB, LANES)) for half in range(2)
        ]

    def halves(ref, item, row):
        return [ref[item, row, :, pl.ds(half * LANES, LANES)] for half in range(2)]

    def start_row(row):
        if isinstance(row, int) and not 0 <= row < rows:
            side, line = (0, row + SUB) if row < 0 else (1, row - rows)
            return [
                [
                    halo.at[side, item, half].reshape(levels * SUB, LANES)[pl.ds(line, levels, stride=SUB), :]
                    for half in range(2)
                ]
                for item in range(3)
            ]
        return [halves(by_row, item, row) for item in range(3)]

    def mid_row(row):
        return [halves(mid, item, row + 1) for item in range(3)]

    def keep_mid(row, carry, rates):
        for item in range(3):
            for half in range(2):
                value = carry[item][half] + 0.5 * time_step * rates[item][half]
                mid[item, row + 1, :, pl.ds(half * LANES, LANES)] = value

    def first_step(carry, row):
        after, rates = advance(carry, start_row(row + 1), fixed_row(0, row + 1), fixed_row(1, row))
        keep_mid(row, carry, rates)
        return after

    def sweep(carry, start, stop, step):
        whole = (stop - start) // UNROLL

        def some(block, carry):
            for extra in range(UNROLL):
                carry = step(carry, start + block * UNROLL + extra)
            return carry

        if whole:
            carry = lax.fori_loop(0, whole, some, carry)
        for row in range(start + whole * UNROLL, stop):
            carry = step(carry, row)
        return carry

    def first_begin(start):
        carry = begin(start_row(start - 1))
        carry, _ = advance(carry, start_row(start), fixed_row(0, start), fixed_row(1, start - 1))
        return carry

    sweep(first_begin(1), 1, rows - 1, first_step)

    out_flat = [[result.at[item, half].reshape(levels * rows, LANES) for half in range(2)] for item in range(3)]

    def second_step(carry, row):
        after, rates = advance(carry, mid_row(row + 1), fixed_row(0, row + 1), fixed_row(1, row))
        start = start_row(row)
        for item in range(3):
            for half in range(2):
                value = 0.5 * (start[item][half] + carry[item][half]) + 0.25 * time_step * rates[item][half]
                out_flat[item][half][pl.ds(row, levels, stride=rows), :] = value
        return after

    def second_sweep(start, stop):
        carry = begin(mid_row(start - 1))
        carry, _ = advance(carry, mid_row(start), fixed_row(0, start), fixed_row(1, start - 1))
        sweep(carry, start, stop, second_step)

    second_sweep(2, rows - 2)

    for copy in along_y:
        copy.wait_recv()

    @pl.when(west_open)
    def _():
        for copy in to_east:
            copy.wait_recv()

    @pl.when(east_open)
    def _():
        for copy in to_west:
            copy.wait_recv()

    sweep(first_begin(-1), -1, 1, first_step)
    sweep(first_begin(rows - 1), rows - 1, rows + 1, first_step)
    second_sweep(0, 2)
    second_sweep(rows - 2, rows)
    for side, after in ((0, 0), (1, rows + SUB)):
        build(lambda item, half, lev: halo[side, item, half, lev], after)

    wide_lane = lax.broadcasted_iota(jnp.int32, (ext, LANES), 1)
    wide_place = wide_lane - (wide_lane // GROUP) * GROUP
    from_west = wide_place < 2
    from_east = wide_place >= 14
    outside = jnp.logical_or(
        jnp.logical_and(from_west, jnp.logical_not(west_open)),
        jnp.logical_and(from_east, jnp.logical_not(east_open)),
    )
    closed = jnp.logical_or(outside, jnp.logical_and(wide_place == 13, jnp.logical_not(east_open)))
    received_west = west_pack[...]
    received_east = east_pack[...]
    fields = []
    for item in range(5):
        value = jnp.where(from_west, turn(received_west, -2 * item), strip[item])
        fields.append(jnp.where(from_east, turn(received_east, 2 * item), value))
    weight = jnp.concatenate([reduced_strip] * (ext // SUB), axis=0)

    def strip_rates(thick, along_x, along_y, bottom, coriolis):
        def north_of(values):
            return pltpu.roll(values, ext - 1, 0)

        def south_of(values):
            return pltpu.roll(values, 1, 0)

        wide = thick + turn(thick, -1)
        flux = wide * along_x
        flux_y = (thick + north_of(thick)) * along_y
        vort = (turn(along_y, -1) - along_y) - (north_of(along_x) - along_x) + coriolis
        spin = quotient(vort, wide + north_of(wide))
        turn_y = spin * (flux_y + turn(flux_y, -1))
        turn_x = spin * (flux + north_of(flux))
        square = along_x * along_x
        square_y = along_y * along_y
        total = thick
        for shift in (16, 32, 64):
            total = total + turn(total, shift)
        bern = 0.5 * ((square + turn(square, 1)) + (square_y + south_of(square_y))) + (bottom + total) + weight * thick
        rate_h = -((flux - turn(flux, 1)) + (flux_y - south_of(flux_y)))
        rate_u = (south_of(turn_y) + turn_y) - (turn(bern, -1) - bern)
        rate_v = -(turn(turn_x, 1) + turn_x) - (north_of(bern) - bern)
        return rate_h, rate_u, rate_v

    rates = strip_rates(*fields)
    middle = []
    for item in range(3):
        value = fields[item] + 0.5 * time_step * rates[item]
        middle.append(jnp.where(closed if item == 1 else outside, 0.0, value))
    rates = strip_rates(*middle, fields[3], fields[4])
    for item in range(3):
        value = 0.5 * (fields[item] + middle[item]) + 0.25 * time_step * rates[item]
        if item == 1:
            value = jnp.where(closed, 0.0, value)
        strip_out[item] = jnp.where(wide_place < 8, turn(value, -6), turn(value, 6))

    for copy in along_y:
        copy.wait_send()

    @pl.when(east_open)
    def _():
        for copy in to_east:
            copy.wait_send()

    @pl.when(west_open)
    def _():
        for copy in to_west:
            copy.wait_send()


def finish(rows, result, strip_out, h_out, vel_out, merged, store_sem):
    levels = SUB
    blocks = rows // SUB
    lane = lax.broadcasted_iota(jnp.int32, (SUB, LANES), 1)

    stores = []
    for block in range(blocks):
        part = pl.ds(block * SUB, SUB)
        for item in range(3):
            value = strip_out[item, pl.ds(block * SUB + SUB, SUB), :]
            for lev in range(levels):
                moved = pltpu.roll(value, (SUB + GROUP * lev) % LANES, 1)
                low = result[item, 0, lev, part, :]
                high = result[item, 1, lev, part, :]
                merged[item, lev, part, pl.ds(0, LANES)] = jnp.where(lane < 2, moved, low)
                merged[item, lev, part, pl.ds(LANES, LANES)] = jnp.where(lane >= LANES - 4, moved, high)
        targets = [h_out.at[:, part], vel_out.at[0, :, part], vel_out.at[1, :, part]]
        for item in range(3):
            copy = pltpu.make_async_copy(merged.at[item, :, part], targets[item], store_sem.at[block, item])
            copy.start()
            stores.append(copy)
    for copy in stores:
        copy.wait()


def solution(mesh):
    count_x, count_y = mesh.shape["gx"], mesh.shape["gy"]

    def body(thickness, velocity, bottom, coriolis, reduced):
        levels, rows, columns = thickness.shape
        assert levels == SUB and columns == 2 * LANES and rows % SUB == 0
        ext = rows + 2 * SUB
        f32 = jnp.float32

        def run(*refs):
            kernel(count_x, count_y, rows, *refs)

        in_hbm = pl.BlockSpec(memory_space=pltpu.HBM)
        in_vmem = pl.BlockSpec(memory_space=pltpu.VMEM)
        result, strip_out = pl.pallas_call(
            run,
            out_shape=(
                pltpu.VMEM((3, 2, levels, rows, LANES), f32),
                pltpu.VMEM((3, ext, LANES), f32),
            ),
            in_specs=[in_hbm] * 5,
            out_specs=(in_vmem, in_vmem),
            scratch_shapes=[
                pltpu.VMEM((3, 2, levels, rows, LANES), f32),
                pltpu.VMEM((3, rows, levels, columns), f32),
                pltpu.VMEM((3, rows + 2, levels, columns), f32),
                pltpu.VMEM((2, 3, 2, levels, SUB, LANES), f32),
                pltpu.VMEM((2, 2, ext, LANES), f32),
                pltpu.VMEM((5, ext, LANES), f32),
                pltpu.VMEM((2, rows, LANES), f32),
                pltpu.VMEM((ext, LANES), f32),
                pltpu.VMEM((ext, LANES), f32),
                pltpu.SMEM((levels,), f32),
                pltpu.SemaphoreType.DMA((2, 3)),
                pltpu.SemaphoreType.DMA((2, 2)),
                pltpu.SemaphoreType.DMA,
                pltpu.SemaphoreType.DMA((3, levels)),
                pltpu.SemaphoreType.DMA((22,)),
                pltpu.SemaphoreType.DMA((22,)),
            ],
            compiler_params=pltpu.CompilerParams(
                collective_id=0, has_side_effects=True, vmem_limit_bytes=VMEM_MAIN
            ),
            cost_estimate=pl.CostEstimate(
                flops=200 * thickness.size, bytes_accessed=28 * thickness.size, transcendentals=0
            ),
        )(thickness, velocity, bottom, coriolis, reduced)

        def end(*refs):
            finish(rows, *refs)

        return pl.pallas_call(
            end,
            out_shape=(
                jax.ShapeDtypeStruct(thickness.shape, f32),
                jax.ShapeDtypeStruct(velocity.shape, f32),
            ),
            in_specs=[in_vmem] * 2,
            out_specs=(in_hbm, in_hbm),
            scratch_shapes=[
                pltpu.VMEM((3, levels, rows, columns), f32),
                pltpu.SemaphoreType.DMA((rows // SUB, 3)),
            ],
            compiler_params=pltpu.CompilerParams(vmem_limit_bytes=VMEM_END),
            cost_estimate=pl.CostEstimate(
                flops=thickness.size, bytes_accessed=24 * thickness.size, transcendentals=0
            ),
        )(result, strip_out)

    return jax.shard_map(
        body,
        mesh=mesh,
        in_specs=(P(None, "gy", "gx"), P(None, None, "gy", "gx"), P("gy", "gx"), P("gy", "gx"), P()),
        out_specs=(P(None, "gy", "gx"), P(None, None, "gy", "gx")),
        check_vma=False,
    )
```

```python
import jax
import jax.numpy as jnp
from jax import lax
from jax.experimental import pallas as pl
from jax.experimental.pallas import tpu as pltpu
from jax.sharding import PartitionSpec as P

time_step = 0.1
LANES = 128
SUB = 8
GROUP = 16
UNROLL = 10
VMEM_MAIN = 58 * 1024 * 1024
VMEM_END = 16 * 1024 * 1024
MESH = pl.DeviceIdType.MESH


def quotient(top, below):
    inverse = pl.reciprocal(below, approx=True)
    return top * (inverse * (2.0 - below * inverse))


def kernel(
    count_x, count_y, rows,
    h_in, vel_in, bottom_in, coriolis_in, reduced_in,
    result, strip_out,
    own, by_row, mid, fixed, strip, pack, west_pack, east_pack,
    reduced_local, load_sem, small_sem, row_sem, send_sem, recv_sem,
):
    levels = SUB
    blocks = rows // SUB
    ext = rows + 2 * SUB
    me_x = lax.axis_index("gx")
    me_y = lax.axis_index("gy")
    west_open = me_x > 0
    east_open = me_x < count_x - 1
    north = lax.rem(me_y + 1, count_y)
    south = lax.rem(me_y + count_y - 1, count_y)

    loads = []
    for half in range(2):
        cols = pl.ds(half * LANES, LANES)
        sources = [h_in.at[:, :, cols], vel_in.at[0, :, :, cols], vel_in.at[1, :, :, cols]]
        for item in range(3):
            loads.append(pltpu.make_async_copy(sources[item], own.at[item, half], load_sem.at[half, item]))
        for item, source in enumerate((bottom_in, coriolis_in)):
            loads.append(
                pltpu.make_async_copy(
                    source.at[:, cols], fixed.at[item, half, pl.ds(SUB, rows)], load_sem.at[half, 3 + item]
                )
            )
    loads.append(pltpu.make_async_copy(reduced_in, reduced_local, small_sem))
    row_loads = []
    for item in range(3):
        for lev in range(levels):
            source = h_in.at[lev] if item == 0 else vel_in.at[item - 1, lev]
            row_loads.append(
                pltpu.make_async_copy(source, by_row.at[item, pl.ds(2, rows), lev], row_sem.at[item, lev])
            )
    for copy in loads + row_loads:
        copy.start()

    barrier = pltpu.get_barrier_semaphore()

    def greet(x, y):
        pl.semaphore_signal(barrier, inc=1, device_id={"gx": x, "gy": y}, device_id_type=MESH)

    greet(me_x, north)
    greet(me_x, south)

    @pl.when(west_open)
    def _():
        for y in (north, me_y, south):
            greet(me_x - 1, y)

    @pl.when(east_open)
    def _():
        for y in (north, me_y, south):
            greet(me_x + 1, y)

    @pl.when(jnp.logical_not(west_open))
    def _():
        west_pack[...] = jnp.zeros_like(west_pack)

    @pl.when(jnp.logical_not(east_open))
    def _():
        east_pack[...] = jnp.zeros_like(east_pack)

    lane = lax.broadcasted_iota(jnp.int32, (SUB, LANES), 1)
    sub = lax.broadcasted_iota(jnp.int32, (SUB, LANES), 0)
    level = levels - 1 - lane // GROUP
    place = lane % GROUP
    for copy in loads:
        copy.wait()
    reduced_main = jnp.zeros((SUB, LANES), jnp.float32)
    reduced_strip = jnp.zeros((SUB, LANES), jnp.float32)
    for item in range(levels):
        value = 2.0 * reduced_local[item]
        reduced_main = jnp.where(sub == item, value, reduced_main)
        reduced_strip = jnp.where(level == item, value, reduced_strip)

    def turn(values, shift):
        return pltpu.roll(values, shift % LANES, 1)

    wall_last = jnp.logical_and(place == 13, jnp.logical_not(east_open))

    def spread(gathered):
        left = turn(gathered, -6)
        right = turn(gathered, 6)
        return jnp.where(place < 8, left, right)

    def build(block, _):
        base = pl.multiple_of(block * SUB, SUB)
        after = pl.multiple_of(block * SUB + SUB, SUB)
        made = []
        for item in range(3):
            gathered = jnp.zeros((SUB, LANES), jnp.float32)
            for lev in range(levels):
                low = own[item, 0, lev, pl.ds(base, SUB), :]
                high = own[item, 1, lev, pl.ds(base, SUB), :]
                joined = jnp.where(lane < LANES // 2, low, high)
                gathered = jnp.where(level == lev, turn(joined, GROUP * (levels - 1 - lev) + 8), gathered)
            value = spread(gathered)
            if item == 1:
                value = jnp.where(wall_last, 0.0, value)
            made.append(value)
        for item in range(2):
            low = fixed[item, 0, pl.ds(after, SUB), :]
            high = fixed[item, 1, pl.ds(after, SUB), :]
            joined = turn(jnp.where(lane < LANES // 2, low, high), 8)
            gathered = jnp.where(lane < GROUP, joined, 0.0)
            for shift in (16, 32, 64):
                gathered = gathered + turn(gathered, shift)
            made.append(spread(gathered))
        for item in range(5):
            strip[item, pl.ds(after, SUB), :] = made[item]
        eastbound = turn(made[4], -4)
        westbound = turn(made[4], 4)
        for item in (3, 2, 1, 0):
            eastbound = jnp.where(place < 2 * item + 2, turn(made[item], 2 * item - 12), eastbound)
            westbound = jnp.where(place >= 14 - 2 * item, turn(made[item], 12 - 2 * item), westbound)
        pack[0, pl.ds(base, SUB), :] = eastbound
        pack[1, pl.ds(base, SUB), :] = westbound
        return 0

    lax.fori_loop(0, blocks, build, 0, unroll=4)
    for copy in row_loads:
        copy.wait()

    first = pl.ds(0, SUB)
    last = pl.ds(rows - SUB, SUB)
    own_first = pl.ds(SUB, 2)
    own_last = pl.ds(rows + SUB - 2, 2)
    ext_south = pl.ds(SUB - 2, 2)
    ext_north = pl.ds(rows + SUB, 2)
    ext_last = pl.ds(rows + SUB, SUB)
    ext_own = pl.ds(SUB, rows)

    def remote(index, source, target, x, y):
        return pltpu.make_async_remote_copy(
            src_ref=source,
            dst_ref=target,
            send_sem=send_sem.at[index],
            recv_sem=recv_sem.at[index],
            device_id={"gx": x, "gy": y},
            device_id_type=MESH,
        )

    along_y = [
        remote(0, by_row.at[:, pl.ds(rows, 2)], by_row.at[:, pl.ds(0, 2)], me_x, north),
        remote(1, by_row.at[:, pl.ds(2, 2)], by_row.at[:, pl.ds(rows + 2, 2)], me_x, south),
        remote(2, fixed.at[:, :, own_last], fixed.at[:, :, ext_south], me_x, north),
        remote(3, fixed.at[:, :, own_first], fixed.at[:, :, ext_north], me_x, south),
        remote(4, strip.at[:, own_last], strip.at[:, ext_south], me_x, north),
        remote(5, strip.at[:, own_first], strip.at[:, ext_north], me_x, south),
    ]
    to_east = [
        remote(6, pack.at[0], west_pack.at[ext_own], me_x + 1, me_y),
        remote(7, pack.at[0, last], west_pack.at[first], me_x + 1, north),
        remote(8, pack.at[0, first], west_pack.at[ext_last], me_x + 1, south),
    ]
    to_west = [
        remote(9, pack.at[1], east_pack.at[ext_own], me_x - 1, me_y),
        remote(10, pack.at[1, last], east_pack.at[first], me_x - 1, north),
        remote(11, pack.at[1, first], east_pack.at[ext_last], me_x - 1, south),
    ]

    greeted = 2 + 3 * west_open.astype(jnp.int32) + 3 * east_open.astype(jnp.int32)
    pl.semaphore_wait(barrier, greeted)
    for copy in along_y:
        copy.start()

    @pl.when(east_open)
    def _():
        for copy in to_east:
            copy.start()

    @pl.when(west_open)
    def _():
        for copy in to_west:
            copy.start()

    before_end = lane < LANES - 1
    at_start = lane == 0

    def eastward(pair):
        low, high = turn(pair[0], -1), turn(pair[1], -1)
        return [jnp.where(before_end, low, high), high]

    def westward(pair):
        low, high = turn(pair[0], 1), turn(pair[1], 1)
        return [low, jnp.where(at_start, low, high)]

    def each(function, *pairs):
        return [function(*items) for items in zip(*pairs)]

    def begin(row):
        thick, along_x, along_y = row
        wide = each(lambda a, b: a + b, thick, eastward(thick))
        flux = each(lambda a, b: a * b, wide, along_x)
        zero = [jnp.zeros((SUB, LANES), jnp.float32)] * 2
        return [thick, along_x, along_y, wide, flux, zero, zero, zero]

    def advance(carry, following, bottom_next, coriolis):
        thick, along_x, along_y, wide, flux, bern, flux_y_before, turn_before = carry
        thick_n, along_x_n, along_y_n = following
        wide_n = each(lambda a, b: a + b, thick_n, eastward(thick_n))
        flux_n = each(lambda a, b: a * b, wide_n, along_x_n)
        flux_y = each(lambda a, b, c: (a + b) * c, thick, thick_n, along_y)
        vort = each(
            lambda e, v, un, u, f: (e - v) - (un - u) + f,
            eastward(along_y), along_y, along_x_n, along_x, coriolis,
        )
        spin = each(lambda z, a, b: quotient(z, a + b), vort, wide, wide_n)
        turn_y = each(lambda w, a, b: w * (a + b), spin, flux_y, eastward(flux_y))
        turn_x = each(lambda w, a, b: w * (a + b), spin, flux, flux_n)
        square = each(lambda a: a * a, along_x_n)
        bern_n = each(
            lambda s, w, vn, v, b, h: 0.5 * ((s + w) + (vn * vn + v * v))
            + (b + jnp.sum(h, axis=0, keepdims=True))
            + reduced_main * h,
            square, westward(square), along_y_n, along_y, bottom_next, thick_n,
        )
        rate_h = each(
            lambda f, w, g, p: -((f - w) + (g - p)), flux, westward(flux), flux_y, flux_y_before
        )
        rate_u = each(lambda p, t, e, b: (p + t) - (e - b), turn_before, turn_y, eastward(bern), bern)
        rate_v = each(lambda w, t, n, b: -(w + t) - (n - b), westward(turn_x), turn_x, bern_n, bern)
        carry = [thick_n, along_x_n, along_y_n, wide_n, flux_n, bern_n, flux_y, turn_y]
        return carry, [rate_h, rate_u, rate_v]

    def fixed_row(item, row):
        return [
            jnp.broadcast_to(fixed[item, half, pl.ds(row + SUB, 1), :], (SUB, LANES)) for half in range(2)
        ]

    def halves(ref, item, row):
        return [ref[item, row, :, pl.ds(half * LANES, LANES)] for half in range(2)]

    def start_row(row):
        return [halves(by_row, item, row + 2) for item in range(3)]

    def mid_row(row):
        return [halves(mid, item, row + 1) for item in range(3)]

    def keep_mid(row, carry, rates):
        for item in range(3):
            for half in range(2):
                value = carry[item][half] + 0.5 * time_step * rates[item][half]
                mid[item, row + 1, :, pl.ds(half * LANES, LANES)] = value

    def first_step(carry, row):
        after, rates = advance(carry, start_row(row + 1), fixed_row(0, row + 1), fixed_row(1, row))
        keep_mid(row, carry, rates)
        return after

    def sweep(carry, start, stop, step):
        whole = (stop - start) // UNROLL

        def some(block, carry):
            for extra in range(UNROLL):
                carry = step(carry, start + block * UNROLL + extra)
            return carry

        if whole:
            carry = lax.fori_loop(0, whole, some, carry)
        for row in range(start + whole * UNROLL, stop):
            carry = step(carry, row)
        return carry

    def first_sweep(start, stop):
        carry = begin(start_row(start - 1))
        carry, _ = advance(carry, start_row(start), fixed_row(0, start), fixed_row(1, start - 1))
        sweep(carry, start, stop, first_step)

    first_sweep(1, rows - 1)

    out_flat = [[result.at[item, half].reshape(levels * rows, LANES) for half in range(2)] for item in range(3)]

    def second_step(carry, row):
        after, rates = advance(carry, mid_row(row + 1), fixed_row(0, row + 1), fixed_row(1, row))
        start = start_row(row)
        for item in range(3):
            for half in range(2):
                value = 0.5 * (start[item][half] + carry[item][half]) + 0.25 * time_step * rates[item][half]
                out_flat[item][half][pl.ds(row, levels, stride=rows), :] = value
        return after

    def second_sweep(start, stop):
        carry = begin(mid_row(start - 1))
        carry, _ = advance(carry, mid_row(start), fixed_row(0, start), fixed_row(1, start - 1))
        sweep(carry, start, stop, second_step)

    second_sweep(2, rows - 2)

    for copy in along_y:
        copy.wait_recv()

    @pl.when(west_open)
    def _():
        for copy in to_east:
            copy.wait_recv()

    @pl.when(east_open)
    def _():
        for copy in to_west:
            copy.wait_recv()

    first_sweep(-1, 1)
    first_sweep(rows - 1, rows + 1)
    second_sweep(0, 2)
    second_sweep(rows - 2, rows)

    wide_lane = lax.broadcasted_iota(jnp.int32, (ext, LANES), 1)
    wide_place = wide_lane - (wide_lane // GROUP) * GROUP
    from_west = wide_place < 2
    from_east = wide_place >= 14
    outside = jnp.logical_or(
        jnp.logical_and(from_west, jnp.logical_not(west_open)),
        jnp.logical_and(from_east, jnp.logical_not(east_open)),
    )
    closed = jnp.logical_or(outside, jnp.logical_and(wide_place == 13, jnp.logical_not(east_open)))
    received_west = west_pack[...]
    received_east = east_pack[...]
    fields = []
    for item in range(5):
        value = jnp.where(from_west, turn(received_west, -2 * item), strip[item])
        fields.append(jnp.where(from_east, turn(received_east, 2 * item), value))
    weight = jnp.concatenate([reduced_strip] * (ext // SUB), axis=0)

    def strip_rates(thick, along_x, along_y, bottom, coriolis):
        def north_of(values):
            return pltpu.roll(values, ext - 1, 0)

        def south_of(values):
            return pltpu.roll(values, 1, 0)

        wide = thick + turn(thick, -1)
        flux = wide * along_x
        flux_y = (thick + north_of(thick)) * along_y
        vort = (turn(along_y, -1) - along_y) - (north_of(along_x) - along_x) + coriolis
        spin = quotient(vort, wide + north_of(wide))
        turn_y = spin * (flux_y + turn(flux_y, -1))
        turn_x = spin * (flux + north_of(flux))
        square = along_x * along_x
        square_y = along_y * along_y
        total = thick
        for shift in (16, 32, 64):
            total = total + turn(total, shift)
        bern = 0.5 * ((square + turn(square, 1)) + (square_y + south_of(square_y))) + (bottom + total) + weight * thick
        rate_h = -((flux - turn(flux, 1)) + (flux_y - south_of(flux_y)))
        rate_u = (south_of(turn_y) + turn_y) - (turn(bern, -1) - bern)
        rate_v = -(turn(turn_x, 1) + turn_x) - (north_of(bern) - bern)
        return rate_h, rate_u, rate_v

    rates = strip_rates(*fields)
    middle = []
    for item in range(3):
        value = fields[item] + 0.5 * time_step * rates[item]
        middle.append(jnp.where(closed if item == 1 else outside, 0.0, value))
    rates = strip_rates(*middle, fields[3], fields[4])
    for item in range(3):
        value = 0.5 * (fields[item] + middle[item]) + 0.25 * time_step * rates[item]
        if item == 1:
            value = jnp.where(closed, 0.0, value)
        strip_out[item] = jnp.where(wide_place < 8, turn(value, -6), turn(value, 6))

    for copy in along_y:
        copy.wait_send()

    @pl.when(east_open)
    def _():
        for copy in to_east:
            copy.wait_send()

    @pl.when(west_open)
    def _():
        for copy in to_west:
            copy.wait_send()


def finish(rows, result, strip_out, h_out, vel_out, merged, store_sem):
    levels = SUB
    blocks = rows // SUB
    lane = lax.broadcasted_iota(jnp.int32, (SUB, LANES), 1)

    stores = []
    for block in range(blocks):
        part = pl.ds(block * SUB, SUB)
        for item in range(3):
            value = strip_out[item, pl.ds(block * SUB + SUB, SUB), :]
            for lev in range(levels):
                moved = pltpu.roll(value, (SUB + GROUP * lev) % LANES, 1)
                low = result[item, 0, lev, part, :]
                high = result[item, 1, lev, part, :]
                merged[item, lev, part, pl.ds(0, LANES)] = jnp.where(lane < 2, moved, low)
                merged[item, lev, part, pl.ds(LANES, LANES)] = jnp.where(lane >= LANES - 4, moved, high)
        targets = [h_out.at[:, part], vel_out.at[0, :, part], vel_out.at[1, :, part]]
        for item in range(3):
            copy = pltpu.make_async_copy(merged.at[item, :, part], targets[item], store_sem.at[block, item])
            copy.start()
            stores.append(copy)
    for copy in stores:
        copy.wait()


def solution(mesh):
    count_x, count_y = mesh.shape["gx"], mesh.shape["gy"]

    def body(thickness, velocity, bottom, coriolis, reduced):
        levels, rows, columns = thickness.shape
        assert levels == SUB and columns == 2 * LANES and rows % SUB == 0
        ext = rows + 2 * SUB
        f32 = jnp.float32

        def run(*refs):
            kernel(count_x, count_y, rows, *refs)

        in_hbm = pl.BlockSpec(memory_space=pltpu.HBM)
        in_vmem = pl.BlockSpec(memory_space=pltpu.VMEM)
        result, strip_out = pl.pallas_call(
            run,
            out_shape=(
                pltpu.VMEM((3, 2, levels, rows, LANES), f32),
                pltpu.VMEM((3, ext, LANES), f32),
            ),
            in_specs=[in_hbm] * 5,
            out_specs=(in_vmem, in_vmem),
            scratch_shapes=[
                pltpu.VMEM((3, 2, levels, rows, LANES), f32),
                pltpu.VMEM((3, rows + 4, levels, columns), f32),
                pltpu.VMEM((3, rows + 2, levels, columns), f32),
                pltpu.VMEM((2, 2, ext, LANES), f32),
                pltpu.VMEM((5, ext, LANES), f32),
                pltpu.VMEM((2, rows, LANES), f32),
                pltpu.VMEM((ext, LANES), f32),
                pltpu.VMEM((ext, LANES), f32),
                pltpu.SMEM((levels,), f32),
                pltpu.SemaphoreType.DMA((2, 5)),
                pltpu.SemaphoreType.DMA,
                pltpu.SemaphoreType.DMA((3, levels)),
                pltpu.SemaphoreType.DMA((12,)),
                pltpu.SemaphoreType.DMA((12,)),
            ],
            compiler_params=pltpu.CompilerParams(
                collective_id=0, has_side_effects=True, vmem_limit_bytes=VMEM_MAIN
            ),
            cost_estimate=pl.CostEstimate(
                flops=200 * thickness.size, bytes_accessed=28 * thickness.size, transcendentals=0
            ),
        )(thickness, velocity, bottom, coriolis, reduced)

        def end(*refs):
            finish(rows, *refs)

        return pl.pallas_call(
            end,
            out_shape=(
                jax.ShapeDtypeStruct(thickness.shape, f32),
                jax.ShapeDtypeStruct(velocity.shape, f32),
            ),
            in_specs=[in_vmem] * 2,
            out_specs=(in_hbm, in_hbm),
            scratch_shapes=[
                pltpu.VMEM((3, levels, rows, columns), f32),
                pltpu.SemaphoreType.DMA((rows // SUB, 3)),
            ],
            compiler_params=pltpu.CompilerParams(vmem_limit_bytes=VMEM_END),
            cost_estimate=pl.CostEstimate(
                flops=thickness.size, bytes_accessed=24 * thickness.size, transcendentals=0
            ),
        )(result, strip_out)

    return jax.shard_map(
        body,
        mesh=mesh,
        in_specs=(P(None, "gy", "gx"), P(None, None, "gy", "gx"), P("gy", "gx"), P("gy", "gx"), P()),
        out_specs=(P(None, "gy", "gx"), P(None, None, "gy", "gx")),
        check_vma=False,
    )
```

```python
import jax
import jax.numpy as jnp
from jax import lax
from jax.experimental import pallas as pl
from jax.experimental.pallas import tpu as pltpu
from jax.sharding import PartitionSpec as P

time_step = 0.1
LANES = 128
SUB = 8
GROUP = 16
UNROLL = 20
VMEM_MAIN = 58 * 1024 * 1024
VMEM_END = 16 * 1024 * 1024
MESH = pl.DeviceIdType.MESH


def quotient(top, below):
    inverse = pl.reciprocal(below, approx=True)
    return top * (inverse * (2.0 - below * inverse))


def kernel(
    count_x, count_y, rows,
    h_in, vel_in, bottom_in, coriolis_in, reduced_in,
    result, strip_out,
    own, by_row, mid, fixed, strip, pack, west_pack, east_pack,
    reduced_local, load_sem, small_sem, row_sem, send_sem, recv_sem,
):
    levels = SUB
    blocks = rows // SUB
    ext = rows + 2 * SUB
    me_x = lax.axis_index("gx")
    me_y = lax.axis_index("gy")
    west_open = me_x > 0
    east_open = me_x < count_x - 1
    north = lax.rem(me_y + 1, count_y)
    south = lax.rem(me_y + count_y - 1, count_y)

    loads = []
    for half in range(2):
        cols = pl.ds(half * LANES, LANES)
        sources = [h_in.at[:, :, cols], vel_in.at[0, :, :, cols], vel_in.at[1, :, :, cols]]
        for item in range(3):
            loads.append(pltpu.make_async_copy(sources[item], own.at[item, half], load_sem.at[half, item]))
        for item, source in enumerate((bottom_in, coriolis_in)):
            loads.append(
                pltpu.make_async_copy(
                    source.at[:, cols], fixed.at[item, half, pl.ds(SUB, rows)], load_sem.at[half, 3 + item]
                )
            )
    loads.append(pltpu.make_async_copy(reduced_in, reduced_local, small_sem))
    row_loads = []
    for item in range(3):
        for lev in range(levels):
            source = h_in.at[lev] if item == 0 else vel_in.at[item - 1, lev]
            row_loads.append(
                pltpu.make_async_copy(source, by_row.at[item, pl.ds(2, rows), lev], row_sem.at[item, lev])
            )
    for copy in loads + row_loads:
        copy.start()

    barrier = pltpu.get_barrier_semaphore()

    def greet(x, y):
        pl.semaphore_signal(barrier, inc=1, device_id={"gx": x, "gy": y}, device_id_type=MESH)

    greet(me_x, north)
    greet(me_x, south)

    @pl.when(west_open)
    def _():
        for y in (north, me_y, south):
            greet(me_x - 1, y)

    @pl.when(east_open)
    def _():
        for y in (north, me_y, south):
            greet(me_x + 1, y)

    @pl.when(jnp.logical_not(west_open))
    def _():
        west_pack[...] = jnp.zeros_like(west_pack)

    @pl.when(jnp.logical_not(east_open))
    def _():
        east_pack[...] = jnp.zeros_like(east_pack)

    lane = lax.broadcasted_iota(jnp.int32, (SUB, LANES), 1)
    sub = lax.broadcasted_iota(jnp.int32, (SUB, LANES), 0)
    level = levels - 1 - lane // GROUP
    place = lane % GROUP
    for copy in loads:
        copy.wait()
    reduced_main = jnp.zeros((SUB, LANES), jnp.float32)
    reduced_strip = jnp.zeros((SUB, LANES), jnp.float32)
    for item in range(levels):
        value = 2.0 * reduced_local[item]
        reduced_main = jnp.where(sub == item, value, reduced_main)
        reduced_strip = jnp.where(level == item, value, reduced_strip)

    def turn(values, shift):
        return pltpu.roll(values, shift % LANES, 1)

    wall_last = jnp.logical_and(place == 13, jnp.logical_not(east_open))

    def spread(gathered):
        left = turn(gathered, -6)
        right = turn(gathered, 6)
        return jnp.where(place < 8, left, right)

    def build(block, _):
        base = pl.multiple_of(block * SUB, SUB)
        after = pl.multiple_of(block * SUB + SUB, SUB)
        made = []
        for item in range(3):
            gathered = jnp.zeros((SUB, LANES), jnp.float32)
            for lev in range(levels):
                low = own[item, 0, lev, pl.ds(base, SUB), :]
                high = own[item, 1, lev, pl.ds(base, SUB), :]
                joined = jnp.where(lane < LANES // 2, low, high)
                gathered = jnp.where(level == lev, turn(joined, GROUP * (levels - 1 - lev) + 8), gathered)
            value = spread(gathered)
            if item == 1:
                value = jnp.where(wall_last, 0.0, value)
            made.append(value)
        for item in range(2):
            low = fixed[item, 0, pl.ds(after, SUB), :]
            high = fixed[item, 1, pl.ds(after, SUB), :]
            joined = turn(jnp.where(lane < LANES // 2, low, high), 8)
            gathered = jnp.where(lane < GROUP, joined, 0.0)
            for shift in (16, 32, 64):
                gathered = gathered + turn(gathered, shift)
            made.append(spread(gathered))
        for item in range(5):
            strip[item, pl.ds(after, SUB), :] = made[item]
        eastbound = turn(made[4], -4)
        westbound = turn(made[4], 4)
        for item in (3, 2, 1, 0):
            eastbound = jnp.where(place < 2 * item + 2, turn(made[item], 2 * item - 12), eastbound)
            westbound = jnp.where(place >= 14 - 2 * item, turn(made[item], 12 - 2 * item), westbound)
        pack[0, pl.ds(base, SUB), :] = eastbound
        pack[1, pl.ds(base, SUB), :] = westbound
        return 0

    lax.fori_loop(0, blocks, build, 0, unroll=4)
    for copy in row_loads:
        copy.wait()

    first = pl.ds(0, SUB)
    last = pl.ds(rows - SUB, SUB)
    own_first = pl.ds(SUB, 2)
    own_last = pl.ds(rows + SUB - 2, 2)
    ext_south = pl.ds(SUB - 2, 2)
    ext_north = pl.ds(rows + SUB, 2)
    ext_last = pl.ds(rows + SUB, SUB)
    ext_own = pl.ds(SUB, rows)

    def remote(index, source, target, x, y):
        return pltpu.make_async_remote_copy(
            src_ref=source,
            dst_ref=target,
            send_sem=send_sem.at[index],
            recv_sem=recv_sem.at[index],
            device_id={"gx": x, "gy": y},
            device_id_type=MESH,
        )

    along_y = [
        remote(0, by_row.at[:, pl.ds(rows, 2)], by_row.at[:, pl.ds(0, 2)], me_x, north),
        remote(1, by_row.at[:, pl.ds(2, 2)], by_row.at[:, pl.ds(rows + 2, 2)], me_x, south),
        remote(2, fixed.at[:, :, own_last], fixed.at[:, :, ext_south], me_x, north),
        remote(3, fixed.at[:, :, own_first], fixed.at[:, :, ext_north], me_x, south),
        remote(4, strip.at[:, own_last], strip.at[:, ext_south], me_x, north),
        remote(5, strip.at[:, own_first], strip.at[:, ext_north], me_x, south),
    ]
    to_east = [
        remote(6, pack.at[0], west_pack.at[ext_own], me_x + 1, me_y),
        remote(7, pack.at[0, last], west_pack.at[first], me_x + 1, north),
        remote(8, pack.at[0, first], west_pack.at[ext_last], me_x + 1, south),
    ]
    to_west = [
        remote(9, pack.at[1], east_pack.at[ext_own], me_x - 1, me_y),
        remote(10, pack.at[1, last], east_pack.at[first], me_x - 1, north),
        remote(11, pack.at[1, first], east_pack.at[ext_last], me_x - 1, south),
    ]

    greeted = 2 + 3 * west_open.astype(jnp.int32) + 3 * east_open.astype(jnp.int32)
    pl.semaphore_wait(barrier, greeted)
    for copy in along_y:
        copy.start()

    @pl.when(east_open)
    def _():
        for copy in to_east:
            copy.start()

    @pl.when(west_open)
    def _():
        for copy in to_west:
            copy.start()

    before_end = lane < LANES - 1
    at_start = lane == 0

    def eastward(pair):
        low, high = turn(pair[0], -1), turn(pair[1], -1)
        return [jnp.where(before_end, low, high), high]

    def westward(pair):
        low, high = turn(pair[0], 1), turn(pair[1], 1)
        return [low, jnp.where(at_start, low, high)]

    def each(function, *pairs):
        return [function(*items) for items in zip(*pairs)]

    def begin(row):
        thick, along_x, along_y = row
        wide = each(lambda a, b: a + b, thick, eastward(thick))
        flux = each(lambda a, b: a * b, wide, along_x)
        zero = [jnp.zeros((SUB, LANES), jnp.float32)] * 2
        return [thick, along_x, along_y, wide, flux, zero, zero, zero]

    def advance(carry, following, bottom_next, coriolis):
        thick, along_x, along_y, wide, flux, bern, flux_y_before, turn_before = carry
        thick_n, along_x_n, along_y_n = following
        wide_n = each(lambda a, b: a + b, thick_n, eastward(thick_n))
        flux_n = each(lambda a, b: a * b, wide_n, along_x_n)
        flux_y = each(lambda a, b, c: (a + b) * c, thick, thick_n, along_y)
        vort = each(
            lambda e, v, un, u, f: (e - v) - (un - u) + f,
            eastward(along_y), along_y, along_x_n, along_x, coriolis,
        )
        spin = each(lambda z, a, b: quotient(z, a + b), vort, wide, wide_n)
        turn_y = each(lambda w, a, b: w * (a + b), spin, flux_y, eastward(flux_y))
        turn_x = each(lambda w, a, b: w * (a + b), spin, flux, flux_n)
        square = each(lambda a: a * a, along_x_n)
        bern_n = each(
            lambda s, w, vn, v, b, h: 0.5 * ((s + w) + (vn * vn + v * v))
            + (b + jnp.sum(h, axis=0, keepdims=True))
            + reduced_main * h,
            square, westward(square), along_y_n, along_y, bottom_next, thick_n,
        )
        rate_h = each(
            lambda f, w, g, p: -((f - w) + (g - p)), flux, westward(flux), flux_y, flux_y_before
        )
        rate_u = each(lambda p, t, e, b: (p + t) - (e - b), turn_before, turn_y, eastward(bern), bern)
        rate_v = each(lambda w, t, n, b: -(w + t) - (n - b), westward(turn_x), turn_x, bern_n, bern)
        carry = [thick_n, along_x_n, along_y_n, wide_n, flux_n, bern_n, flux_y, turn_y]
        return carry, [rate_h, rate_u, rate_v]

    def fixed_row(item, row):
        return [
            jnp.broadcast_to(fixed[item, half, pl.ds(row + SUB, 1), :], (SUB, LANES)) for half in range(2)
        ]

    def halves(ref, item, row):
        return [ref[item, row, :, pl.ds(half * LANES, LANES)] for half in range(2)]

    def start_row(row):
        return [halves(by_row, item, row + 2) for item in range(3)]

    def mid_row(row):
        return [halves(mid, item, row + 1) for item in range(3)]

    def keep_mid(row, carry, rates):
        for item in range(3):
            for half in range(2):
                value = carry[item][half] + 0.5 * time_step * rates[item][half]
                mid[item, row + 1, :, pl.ds(half * LANES, LANES)] = value

    def first_step(carry, row):
        after, rates = advance(carry, start_row(row + 1), fixed_row(0, row + 1), fixed_row(1, row))
        keep_mid(row, carry, rates)
        return after

    def sweep(carry, start, stop, step):
        whole = (stop - start) // UNROLL

        def some(block, carry):
            for extra in range(UNROLL):
                carry = step(carry, start + block * UNROLL + extra)
            return carry

        if whole:
            carry = lax.fori_loop(0, whole, some, carry)
        for row in range(start + whole * UNROLL, stop):
            carry = step(carry, row)
        return carry

    def first_sweep(start, stop):
        carry = begin(start_row(start - 1))
        carry, _ = advance(carry, start_row(start), fixed_row(0, start), fixed_row(1, start - 1))
        sweep(carry, start, stop, first_step)

    first_sweep(1, rows - 1)

    out_flat = [[result.at[item, half].reshape(levels * rows, LANES) for half in range(2)] for item in range(3)]

    def second_step(carry, row):
        after, rates = advance(carry, mid_row(row + 1), fixed_row(0, row + 1), fixed_row(1, row))
        start = start_row(row)
        for item in range(3):
            for half in range(2):
                value = 0.5 * (start[item][half] + carry[item][half]) + 0.25 * time_step * rates[item][half]
                out_flat[item][half][pl.ds(row, levels, stride=rows), :] = value
        return after

    def second_sweep(start, stop):
        carry = begin(mid_row(start - 1))
        carry, _ = advance(carry, mid_row(start), fixed_row(0, start), fixed_row(1, start - 1))
        sweep(carry, start, stop, second_step)

    second_sweep(2, rows - 2)

    for copy in along_y:
        copy.wait_recv()

    @pl.when(west_open)
    def _():
        for copy in to_east:
            copy.wait_recv()

    @pl.when(east_open)
    def _():
        for copy in to_west:
            copy.wait_recv()

    first_sweep(-1, 1)
    first_sweep(rows - 1, rows + 1)
    second_sweep(0, 2)
    second_sweep(rows - 2, rows)

    wide_lane = lax.broadcasted_iota(jnp.int32, (ext, LANES), 1)
    wide_place = wide_lane - (wide_lane // GROUP) * GROUP
    from_west = wide_place < 2
    from_east = wide_place >= 14
    outside = jnp.logical_or(
        jnp.logical_and(from_west, jnp.logical_not(west_open)),
        jnp.logical_and(from_east, jnp.logical_not(east_open)),
    )
    closed = jnp.logical_or(outside, jnp.logical_and(wide_place == 13, jnp.logical_not(east_open)))
    received_west = west_pack[...]
    received_east = east_pack[...]
    fields = []
    for item in range(5):
        value = jnp.where(from_west, turn(received_west, -2 * item), strip[item])
        fields.append(jnp.where(from_east, turn(received_east, 2 * item), value))
    weight = jnp.concatenate([reduced_strip] * (ext // SUB), axis=0)

    def strip_rates(thick, along_x, along_y, bottom, coriolis):
        def north_of(values):
            return pltpu.roll(values, ext - 1, 0)

        def south_of(values):
            return pltpu.roll(values, 1, 0)

        wide = thick + turn(thick, -1)
        flux = wide * along_x
        flux_y = (thick + north_of(thick)) * along_y
        vort = (turn(along_y, -1) - along_y) - (north_of(along_x) - along_x) + coriolis
        spin = quotient(vort, wide + north_of(wide))
        turn_y = spin * (flux_y + turn(flux_y, -1))
        turn_x = spin * (flux + north_of(flux))
        square = along_x * along_x
        square_y = along_y * along_y
        total = thick
        for shift in (16, 32, 64):
            total = total + turn(total, shift)
        bern = 0.5 * ((square + turn(square, 1)) + (square_y + south_of(square_y))) + (bottom + total) + weight * thick
        rate_h = -((flux - turn(flux, 1)) + (flux_y - south_of(flux_y)))
        rate_u = (south_of(turn_y) + turn_y) - (turn(bern, -1) - bern)
        rate_v = -(turn(turn_x, 1) + turn_x) - (north_of(bern) - bern)
        return rate_h, rate_u, rate_v

    rates = strip_rates(*fields)
    middle = []
    for item in range(3):
        value = fields[item] + 0.5 * time_step * rates[item]
        middle.append(jnp.where(closed if item == 1 else outside, 0.0, value))
    rates = strip_rates(*middle, fields[3], fields[4])
    for item in range(3):
        value = 0.5 * (fields[item] + middle[item]) + 0.25 * time_step * rates[item]
        if item == 1:
            value = jnp.where(closed, 0.0, value)
        strip_out[item] = jnp.where(wide_place < 8, turn(value, -6), turn(value, 6))

    for copy in along_y:
        copy.wait_send()

    @pl.when(east_open)
    def _():
        for copy in to_east:
            copy.wait_send()

    @pl.when(west_open)
    def _():
        for copy in to_west:
            copy.wait_send()


def finish(rows, result, strip_out, h_out, vel_out, merged, store_sem):
    levels = SUB
    blocks = rows // SUB
    lane = lax.broadcasted_iota(jnp.int32, (SUB, LANES), 1)

    stores = []
    for block in range(blocks):
        part = pl.ds(block * SUB, SUB)
        for item in range(3):
            value = strip_out[item, pl.ds(block * SUB + SUB, SUB), :]
            for lev in range(levels):
                moved = pltpu.roll(value, (SUB + GROUP * lev) % LANES, 1)
                low = result[item, 0, lev, part, :]
                high = result[item, 1, lev, part, :]
                merged[item, lev, part, pl.ds(0, LANES)] = jnp.where(lane < 2, moved, low)
                merged[item, lev, part, pl.ds(LANES, LANES)] = jnp.where(lane >= LANES - 4, moved, high)
        targets = [h_out.at[:, part], vel_out.at[0, :, part], vel_out.at[1, :, part]]
        for item in range(3):
            copy = pltpu.make_async_copy(merged.at[item, :, part], targets[item], store_sem.at[block, item])
            copy.start()
            stores.append(copy)
    for copy in stores:
        copy.wait()


def solution(mesh):
    count_x, count_y = mesh.shape["gx"], mesh.shape["gy"]

    def body(thickness, velocity, bottom, coriolis, reduced):
        levels, rows, columns = thickness.shape
        assert levels == SUB and columns == 2 * LANES and rows % SUB == 0
        ext = rows + 2 * SUB
        f32 = jnp.float32

        def run(*refs):
            kernel(count_x, count_y, rows, *refs)

        in_hbm = pl.BlockSpec(memory_space=pltpu.HBM)
        in_vmem = pl.BlockSpec(memory_space=pltpu.VMEM)
        result, strip_out = pl.pallas_call(
            run,
            out_shape=(
                pltpu.VMEM((3, 2, levels, rows, LANES), f32),
                pltpu.VMEM((3, ext, LANES), f32),
            ),
            in_specs=[in_hbm] * 5,
            out_specs=(in_vmem, in_vmem),
            scratch_shapes=[
                pltpu.VMEM((3, 2, levels, rows, LANES), f32),
                pltpu.VMEM((3, rows + 4, levels, columns), f32),
                pltpu.VMEM((3, rows + 2, levels, columns), f32),
                pltpu.VMEM((2, 2, ext, LANES), f32),
                pltpu.VMEM((5, ext, LANES), f32),
                pltpu.VMEM((2, rows, LANES), f32),
                pltpu.VMEM((ext, LANES), f32),
                pltpu.VMEM((ext, LANES), f32),
                pltpu.SMEM((levels,), f32),
                pltpu.SemaphoreType.DMA((2, 5)),
                pltpu.SemaphoreType.DMA,
                pltpu.SemaphoreType.DMA((3, levels)),
                pltpu.SemaphoreType.DMA((12,)),
                pltpu.SemaphoreType.DMA((12,)),
            ],
            compiler_params=pltpu.CompilerParams(
                collective_id=0, has_side_effects=True, vmem_limit_bytes=VMEM_MAIN
            ),
            cost_estimate=pl.CostEstimate(
                flops=200 * thickness.size, bytes_accessed=28 * thickness.size, transcendentals=0
            ),
        )(thickness, velocity, bottom, coriolis, reduced)

        def end(*refs):
            finish(rows, *refs)

        return pl.pallas_call(
            end,
            out_shape=(
                jax.ShapeDtypeStruct(thickness.shape, f32),
                jax.ShapeDtypeStruct(velocity.shape, f32),
            ),
            in_specs=[in_vmem] * 2,
            out_specs=(in_hbm, in_hbm),
            scratch_shapes=[
                pltpu.VMEM((3, levels, rows, columns), f32),
                pltpu.SemaphoreType.DMA((rows // SUB, 3)),
            ],
            compiler_params=pltpu.CompilerParams(vmem_limit_bytes=VMEM_END),
            cost_estimate=pl.CostEstimate(
                flops=thickness.size, bytes_accessed=24 * thickness.size, transcendentals=0
            ),
        )(result, strip_out)

    return jax.shard_map(
        body,
        mesh=mesh,
        in_specs=(P(None, "gy", "gx"), P(None, None, "gy", "gx"), P("gy", "gx"), P("gy", "gx"), P()),
        out_specs=(P(None, "gy", "gx"), P(None, None, "gy", "gx")),
        check_vma=False,
    )
```

```python
import jax
import jax.numpy as jnp
from jax import lax
from jax.experimental import pallas as pl
from jax.experimental.pallas import tpu as pltpu
from jax.sharding import PartitionSpec as P

time_step = 0.1
LANES = 128
SUB = 8
GROUP = 16
UNROLL = 6
VMEM_MAIN = 58 * 1024 * 1024
VMEM_END = 16 * 1024 * 1024
MESH = pl.DeviceIdType.MESH


def quotient(top, below):
    inverse = pl.reciprocal(below, approx=True)
    return top * (inverse * (2.0 - below * inverse))


def kernel(
    count_x, count_y, rows,
    h_in, vel_in, bottom_in, coriolis_in, reduced_in,
    result, strip_out,
    own, by_row, mid, fixed, strip, pack, west_pack, east_pack,
    reduced_local, load_sem, small_sem, row_sem, send_sem, recv_sem,
):
    levels = SUB
    blocks = rows // SUB
    ext = rows + 2 * SUB
    me_x = lax.axis_index("gx")
    me_y = lax.axis_index("gy")
    west_open = me_x > 0
    east_open = me_x < count_x - 1
    north = lax.rem(me_y + 1, count_y)
    south = lax.rem(me_y + count_y - 1, count_y)

    loads = []
    for half in range(2):
        cols = pl.ds(half * LANES, LANES)
        sources = [h_in.at[:, :, cols], vel_in.at[0, :, :, cols], vel_in.at[1, :, :, cols]]
        for item in range(3):
            loads.append(pltpu.make_async_copy(sources[item], own.at[item, half], load_sem.at[half, item]))
        for item, source in enumerate((bottom_in, coriolis_in)):
            loads.append(
                pltpu.make_async_copy(
                    source.at[:, cols], fixed.at[item, half, pl.ds(SUB, rows)], load_sem.at[half, 3 + item]
                )
            )
    loads.append(pltpu.make_async_copy(reduced_in, reduced_local, small_sem))
    row_loads = []
    for item in range(3):
        for lev in range(levels):
            source = h_in.at[lev] if item == 0 else vel_in.at[item - 1, lev]
            row_loads.append(
                pltpu.make_async_copy(source, by_row.at[item, pl.ds(2, rows), lev], row_sem.at[item, lev])
            )
    for copy in loads + row_loads:
        copy.start()

    barrier = pltpu.get_barrier_semaphore()

    def greet(x, y):
        pl.semaphore_signal(barrier, inc=1, device_id={"gx": x, "gy": y}, device_id_type=MESH)

    greet(me_x, north)
    greet(me_x, south)

    @pl.when(west_open)
    def _():
        for y in (north, me_y, south):
            greet(me_x - 1, y)

    @pl.when(east_open)
    def _():
        for y in (north, me_y, south):
            greet(me_x + 1, y)

    @pl.when(jnp.logical_not(west_open))
    def _():
        west_pack[...] = jnp.zeros_like(west_pack)

    @pl.when(jnp.logical_not(east_open))
    def _():
        east_pack[...] = jnp.zeros_like(east_pack)

    lane = lax.broadcasted_iota(jnp.int32, (SUB, LANES), 1)
    sub = lax.broadcasted_iota(jnp.int32, (SUB, LANES), 0)
    level = levels - 1 - lane // GROUP
    place = lane % GROUP
    for copy in loads:
        copy.wait()
    reduced_main = jnp.zeros((SUB, LANES), jnp.float32)
    reduced_strip = jnp.zeros((SUB, LANES), jnp.float32)
    for item in range(levels):
        value = 2.0 * reduced_local[item]
        reduced_main = jnp.where(sub == item, value, reduced_main)
        reduced_strip = jnp.where(level == item, value, reduced_strip)

    def turn(values, shift):
        return pltpu.roll(values, shift % LANES, 1)

    wall_last = jnp.logical_and(place == 13, jnp.logical_not(east_open))

    def spread(gathered):
        left = turn(gathered, -6)
        right = turn(gathered, 6)
        return jnp.where(place < 8, left, right)

    def build(block, _):
        base = pl.multiple_of(block * SUB, SUB)
        after = pl.multiple_of(block * SUB + SUB, SUB)
        made = []
        for item in range(3):
            gathered = jnp.zeros((SUB, LANES), jnp.float32)
            for lev in range(levels):
                low = own[item, 0, lev, pl.ds(base, SUB), :]
                high = own[item, 1, lev, pl.ds(base, SUB), :]
                joined = jnp.where(lane < LANES // 2, low, high)
                gathered = jnp.where(level == lev, turn(joined, GROUP * (levels - 1 - lev) + 8), gathered)
            value = spread(gathered)
            if item == 1:
                value = jnp.where(wall_last, 0.0, value)
            made.append(value)
        for item in range(2):
            low = fixed[item, 0, pl.ds(after, SUB), :]
            high = fixed[item, 1, pl.ds(after, SUB), :]
            joined = turn(jnp.where(lane < LANES // 2, low, high), 8)
            gathered = jnp.where(lane < GROUP, joined, 0.0)
            for shift in (16, 32, 64):
                gathered = gathered + turn(gathered, shift)
            made.append(spread(gathered))
        for item in range(5):
            strip[item, pl.ds(after, SUB), :] = made[item]
        eastbound = turn(made[4], -4)
        westbound = turn(made[4], 4)
        for item in (3, 2, 1, 0):
            eastbound = jnp.where(place < 2 * item + 2, turn(made[item], 2 * item - 12), eastbound)
            westbound = jnp.where(place >= 14 - 2 * item, turn(made[item], 12 - 2 * item), westbound)
        pack[0, pl.ds(base, SUB), :] = eastbound
        pack[1, pl.ds(base, SUB), :] = westbound
        return 0

    lax.fori_loop(0, blocks, build, 0, unroll=4)
    for copy in row_loads:
        copy.wait()

    first = pl.ds(0, SUB)
    last = pl.ds(rows - SUB, SUB)
    own_first = pl.ds(SUB, 2)
    own_last = pl.ds(rows + SUB - 2, 2)
    ext_south = pl.ds(SUB - 2, 2)
    ext_north = pl.ds(rows + SUB, 2)
    ext_last = pl.ds(rows + SUB, SUB)
    ext_own = pl.ds(SUB, rows)

    def remote(index, source, target, x, y):
        return pltpu.make_async_remote_copy(
            src_ref=source,
            dst_ref=target,
            send_sem=send_sem.at[index],
            recv_sem=recv_sem.at[index],
            device_id={"gx": x, "gy": y},
            device_id_type=MESH,
        )

    along_y = [
        remote(0, by_row.at[:, pl.ds(rows, 2)], by_row.at[:, pl.ds(0, 2)], me_x, north),
        remote(1, by_row.at[:, pl.ds(2, 2)], by_row.at[:, pl.ds(rows + 2, 2)], me_x, south),
        remote(2, fixed.at[:, :, own_last], fixed.at[:, :, ext_south], me_x, north),
        remote(3, fixed.at[:, :, own_first], fixed.at[:, :, ext_north], me_x, south),
        remote(4, strip.at[:, own_last], strip.at[:, ext_south], me_x, north),
        remote(5, strip.at[:, own_first], strip.at[:, ext_north], me_x, south),
    ]
    to_east = [
        remote(6, pack.at[0], west_pack.at[ext_own], me_x + 1, me_y),
        remote(7, pack.at[0, last], west_pack.at[first], me_x + 1, north),
        remote(8, pack.at[0, first], west_pack.at[ext_last], me_x + 1, south),
    ]
    to_west = [
        remote(9, pack.at[1], east_pack.at[ext_own], me_x - 1, me_y),
        remote(10, pack.at[1, last], east_pack.at[first], me_x - 1, north),
        remote(11, pack.at[1, first], east_pack.at[ext_last], me_x - 1, south),
    ]

    greeted = 2 + 3 * west_open.astype(jnp.int32) + 3 * east_open.astype(jnp.int32)
    pl.semaphore_wait(barrier, greeted)
    for copy in along_y:
        copy.start()

    @pl.when(east_open)
    def _():
        for copy in to_east:
            copy.start()

    @pl.when(west_open)
    def _():
        for copy in to_west:
            copy.start()

    before_end = lane < LANES - 1
    at_start = lane == 0

    def eastward(pair):
        low, high = turn(pair[0], -1), turn(pair[1], -1)
        return [jnp.where(before_end, low, high), high]

    def westward(pair):
        low, high = turn(pair[0], 1), turn(pair[1], 1)
        return [low, jnp.where(at_start, low, high)]

    def each(function, *pairs):
        return [function(*items) for items in zip(*pairs)]

    def begin(row):
        thick, along_x, along_y = row
        wide = each(lambda a, b: a + b, thick, eastward(thick))
        flux = each(lambda a, b: a * b, wide, along_x)
        zero = [jnp.zeros((SUB, LANES), jnp.float32)] * 2
        return [thick, along_x, along_y, wide, flux, zero, zero, zero]

    def advance(carry, following, bottom_next, coriolis):
        thick, along_x, along_y, wide, flux, bern, flux_y_before, turn_before = carry
        thick_n, along_x_n, along_y_n = following
        wide_n = each(lambda a, b: a + b, thick_n, eastward(thick_n))
        flux_n = each(lambda a, b: a * b, wide_n, along_x_n)
        flux_y = each(lambda a, b, c: (a + b) * c, thick, thick_n, along_y)
        vort = each(
            lambda e, v, un, u, f: (e - v) - (un - u) + f,
            eastward(along_y), along_y, along_x_n, along_x, coriolis,
        )
        spin = each(lambda z, a, b: quotient(z, a + b), vort, wide, wide_n)
        turn_y = each(lambda w, a, b: w * (a + b), spin, flux_y, eastward(flux_y))
        turn_x = each(lambda w, a, b: w * (a + b), spin, flux, flux_n)
        square = each(lambda a: a * a, along_x_n)
        bern_n = each(
            lambda s, w, vn, v, b, h: 0.5 * ((s + w) + (vn * vn + v * v))
            + (b + jnp.sum(h, axis=0, keepdims=True))
            + reduced_main * h,
            square, westward(square), along_y_n, along_y, bottom_next, thick_n,
        )
        rate_h = each(
            lambda f, w, g, p: -((f - w) + (g - p)), flux, westward(flux), flux_y, flux_y_before
        )
        rate_u = each(lambda p, t, e, b: (p + t) - (e - b), turn_before, turn_y, eastward(bern), bern)
        rate_v = each(lambda w, t, n, b: -(w + t) - (n - b), westward(turn_x), turn_x, bern_n, bern)
        carry = [thick_n, along_x_n, along_y_n, wide_n, flux_n, bern_n, flux_y, turn_y]
        return carry, [rate_h, rate_u, rate_v]

    def fixed_row(item, row):
        return [
            jnp.broadcast_to(fixed[item, half, pl.ds(row + SUB, 1), :], (SUB, LANES)) for half in range(2)
        ]

    def halves(ref, item, row):
        return [ref[item, row, :, pl.ds(half * LANES, LANES)] for half in range(2)]

    def start_row(row):
        return [halves(by_row, item, row + 2) for item in range(3)]

    def mid_row(row):
        return [halves(mid, item, row + 1) for item in range(3)]

    def keep_mid(row, carry, rates):
        for item in range(3):
            for half in range(2):
                value = carry[item][half] + 0.5 * time_step * rates[item][half]
                mid[item, row + 1, :, pl.ds(half * LANES, LANES)] = value

    def first_step(carry, row):
        after, rates = advance(carry, start_row(row + 1), fixed_row(0, row + 1), fixed_row(1, row))
        keep_mid(row, carry, rates)
        return after

    def sweep(carry, start, stop, step):
        whole = (stop - start) // UNROLL

        def some(block, carry):
            for extra in range(UNROLL):
                carry = step(carry, start + block * UNROLL + extra)
            return carry

        if whole:
            carry = lax.fori_loop(0, whole, some, carry)
        for row in range(start + whole * UNROLL, stop):
            carry = step(carry, row)
        return carry

    def first_begin(start):
        carry = begin(start_row(start - 1))
        carry, _ = advance(carry, start_row(start), fixed_row(0, start), fixed_row(1, start - 1))
        return carry

    sweep(first_begin(1), 1, rows - 1, first_step)

    out_flat = [[result.at[item, half].reshape(levels * rows, LANES) for half in range(2)] for item in range(3)]

    def second_step(carry, row):
        after, rates = advance(carry, mid_row(row + 1), fixed_row(0, row + 1), fixed_row(1, row))
        start = start_row(row)
        for item in range(3):
            for half in range(2):
                value = 0.5 * (start[item][half] + carry[item][half]) + 0.25 * time_step * rates[item][half]
                out_flat[item][half][pl.ds(row, levels, stride=rows), :] = value
        return after

    def second_begin(start):
        carry = begin(mid_row(start - 1))
        carry, _ = advance(carry, mid_row(start), fixed_row(0, start), fixed_row(1, start - 1))
        return carry

    sweep(second_begin(2), 2, rows - 2, second_step)

    for copy in along_y:
        copy.wait_recv()

    @pl.when(west_open)
    def _():
        for copy in to_east:
            copy.wait_recv()

    @pl.when(east_open)
    def _():
        for copy in to_west:
            copy.wait_recv()


    def first_edge(side, _):
        start = side * rows - 1
        carry = first_begin(start)
        for step in range(2):
            carry = first_step(carry, start + step)
        return 0

    def second_edge(side, _):
        start = side * (rows - 2)
        carry = second_begin(start)
        for step in range(2):
            carry = second_step(carry, start + step)
        return 0

    lax.fori_loop(0, 2, first_edge, 0)
    lax.fori_loop(0, 2, second_edge, 0)

    wide_lane = lax.broadcasted_iota(jnp.int32, (ext, LANES), 1)
    wide_place = wide_lane - (wide_lane // GROUP) * GROUP
    from_west = wide_place < 2
    from_east = wide_place >= 14
    outside = jnp.logical_or(
        jnp.logical_and(from_west, jnp.logical_not(west_open)),
        jnp.logical_and(from_east, jnp.logical_not(east_open)),
    )
    closed = jnp.logical_or(outside, jnp.logical_and(wide_place == 13, jnp.logical_not(east_open)))
    received_west = west_pack[...]
    received_east = east_pack[...]
    fields = []
    for item in range(5):
        value = jnp.where(from_west, turn(received_west, -2 * item), strip[item])
        fields.append(jnp.where(from_east, turn(received_east, 2 * item), value))
    weight = jnp.concatenate([reduced_strip] * (ext // SUB), axis=0)

    def strip_rates(thick, along_x, along_y, bottom, coriolis):
        def north_of(values):
            return pltpu.roll(values, ext - 1, 0)

        def south_of(values):
            return pltpu.roll(values, 1, 0)

        wide = thick + turn(thick, -1)
        flux = wide * along_x
        flux_y = (thick + north_of(thick)) * along_y
        vort = (turn(along_y, -1) - along_y) - (north_of(along_x) - along_x) + coriolis
        spin = quotient(vort, wide + north_of(wide))
        turn_y = spin * (flux_y + turn(flux_y, -1))
        turn_x = spin * (flux + north_of(flux))
        square = along_x * along_x
        square_y = along_y * along_y
        total = thick
        for shift in (16, 32, 64):
            total = total + turn(total, shift)
        bern = 0.5 * ((square + turn(square, 1)) + (square_y + south_of(square_y))) + (bottom + total) + weight * thick
        rate_h = -((flux - turn(flux, 1)) + (flux_y - south_of(flux_y)))
        rate_u = (south_of(turn_y) + turn_y) - (turn(bern, -1) - bern)
        rate_v = -(turn(turn_x, 1) + turn_x) - (north_of(bern) - bern)
        return rate_h, rate_u, rate_v

    rates = strip_rates(*fields)
    middle = []
    for item in range(3):
        value = fields[item] + 0.5 * time_step * rates[item]
        middle.append(jnp.where(closed if item == 1 else outside, 0.0, value))
    rates = strip_rates(*middle, fields[3], fields[4])
    for item in range(3):
        value = 0.5 * (fields[item] + middle[item]) + 0.25 * time_step * rates[item]
        if item == 1:
            value = jnp.where(closed, 0.0, value)
        strip_out[item] = jnp.where(wide_place < 8, turn(value, -6), turn(value, 6))

    for copy in along_y:
        copy.wait_send()

    @pl.when(east_open)
    def _():
        for copy in to_east:
            copy.wait_send()

    @pl.when(west_open)
    def _():
        for copy in to_west:
            copy.wait_send()


def finish(rows, result, strip_out, h_out, vel_out, merged, store_sem):
    levels = SUB
    blocks = rows // SUB
    lane = lax.broadcasted_iota(jnp.int32, (SUB, LANES), 1)

    stores = []
    for block in range(blocks):
        part = pl.ds(block * SUB, SUB)
        for item in range(3):
            value = strip_out[item, pl.ds(block * SUB + SUB, SUB), :]
            for lev in range(levels):
                moved = pltpu.roll(value, (SUB + GROUP * lev) % LANES, 1)
                low = result[item, 0, lev, part, :]
                high = result[item, 1, lev, part, :]
                merged[item, lev, part, pl.ds(0, LANES)] = jnp.where(lane < 2, moved, low)
                merged[item, lev, part, pl.ds(LANES, LANES)] = jnp.where(lane >= LANES - 4, moved, high)
        targets = [h_out.at[:, part], vel_out.at[0, :, part], vel_out.at[1, :, part]]
        for item in range(3):
            copy = pltpu.make_async_copy(merged.at[item, :, part], targets[item], store_sem.at[block, item])
            copy.start()
            stores.append(copy)
    for copy in stores:
        copy.wait()


def solution(mesh):
    count_x, count_y = mesh.shape["gx"], mesh.shape["gy"]

    def body(thickness, velocity, bottom, coriolis, reduced):
        levels, rows, columns = thickness.shape
        assert levels == SUB and columns == 2 * LANES and rows % SUB == 0
        ext = rows + 2 * SUB
        f32 = jnp.float32

        def run(*refs):
            kernel(count_x, count_y, rows, *refs)

        in_hbm = pl.BlockSpec(memory_space=pltpu.HBM)
        in_vmem = pl.BlockSpec(memory_space=pltpu.VMEM)
        result, strip_out = pl.pallas_call(
            run,
            out_shape=(
                pltpu.VMEM((3, 2, levels, rows, LANES), f32),
                pltpu.VMEM((3, ext, LANES), f32),
            ),
            in_specs=[in_hbm] * 5,
            out_specs=(in_vmem, in_vmem),
            scratch_shapes=[
                pltpu.VMEM((3, 2, levels, rows, LANES), f32),
                pltpu.VMEM((3, rows + 4, levels, columns), f32),
                pltpu.VMEM((3, rows + 2, levels, columns), f32),
                pltpu.VMEM((2, 2, ext, LANES), f32),
                pltpu.VMEM((5, ext, LANES), f32),
                pltpu.VMEM((2, rows, LANES), f32),
                pltpu.VMEM((ext, LANES), f32),
                pltpu.VMEM((ext, LANES), f32),
                pltpu.SMEM((levels,), f32),
                pltpu.SemaphoreType.DMA((2, 5)),
                pltpu.SemaphoreType.DMA,
                pltpu.SemaphoreType.DMA((3, levels)),
                pltpu.SemaphoreType.DMA((12,)),
                pltpu.SemaphoreType.DMA((12,)),
            ],
            compiler_params=pltpu.CompilerParams(
                collective_id=0, has_side_effects=True, vmem_limit_bytes=VMEM_MAIN
            ),
            cost_estimate=pl.CostEstimate(
                flops=200 * thickness.size, bytes_accessed=28 * thickness.size, transcendentals=0
            ),
        )(thickness, velocity, bottom, coriolis, reduced)

        def end(*refs):
            finish(rows, *refs)

        return pl.pallas_call(
            end,
            out_shape=(
                jax.ShapeDtypeStruct(thickness.shape, f32),
                jax.ShapeDtypeStruct(velocity.shape, f32),
            ),
            in_specs=[in_vmem] * 2,
            out_specs=(in_hbm, in_hbm),
            scratch_shapes=[
                pltpu.VMEM((3, levels, rows, columns), f32),
                pltpu.SemaphoreType.DMA((rows // SUB, 3)),
            ],
            compiler_params=pltpu.CompilerParams(vmem_limit_bytes=VMEM_END),
            cost_estimate=pl.CostEstimate(
                flops=thickness.size, bytes_accessed=24 * thickness.size, transcendentals=0
            ),
        )(result, strip_out)

    return jax.shard_map(
        body,
        mesh=mesh,
        in_specs=(P(None, "gy", "gx"), P(None, None, "gy", "gx"), P("gy", "gx"), P("gy", "gx"), P()),
        out_specs=(P(None, "gy", "gx"), P(None, None, "gy", "gx")),
        check_vma=False,
    )
```
